256 devices in a mesh: dp: 4 (over x_lo, core), expert: 64 (over y, x_hi, z).
Axes of the slice: x: 4 (x_hi: 2, x_lo: 2; x = x_hi * 2 + x_lo), y: 4, z: 8, core: 2. Of those that a mesh axis runs over, the one named last changes fastest.
Arguments:
- tokens: bfloat16 [512, 256, 1280], P(('dp', 'expert')), may hold values from -48 to 48
- cotangent: bfloat16 [512, 256, 1280], P(('dp', 'expert')), may hold values from -6 to 6
- router: bfloat16 [1280, 64], replicated, may hold values from -1 to 1
- first_weight: bfloat16 [64, 1280, 2560], P('expert', None, 'dp'), may hold values from -0.15625 to 0.15625
- second_weight: bfloat16 [64, 2560, 1280], P('expert', 'dp'), may hold values from -0.125 to 0.125
Outputs:
- token_grad: bfloat16 [512, 256, 1280], P(('dp', 'expert'))
- router_grad: float32 [1280, 64], P(None, 'expert')
- first_grad: bfloat16 [64, 1280, 2560], P('expert', None, 'dp')
- second_grad: bfloat16 [64, 2560, 1280], P('expert', 'dp')
The draws below stay inside these ranges and needn't reach their ends.
All inputs are finite; a program needn't handle non-finite values.
Results may differ from the reference program's by a relative error of at most 0.018.
Values may be sent and summed in bfloat16 or wider, within the bound.
A program may use at most 128 MiB of HBM per device.

```python
import jax
import jax.numpy as jnp
from jax import lax

D = 1280
PATCHES = 256
EXP_HIDDEN = 2560
EXPERTS = 64
IMAGES = 512
N_DP = 4


def router_table(key):
    return jax.random.normal(key, (D, EXPERTS), jnp.float32) * D ** (-0.5)


def draw_router(key, part):
    return router_table(key).astype(jnp.bfloat16)


def draw_tokens(key, part):
    key = jax.random.fold_in(key, 5)
    noise_key = jax.random.fold_in(key, 0)
    base = jnp.clip(jax.random.normal(noise_key, (IMAGES, PATCHES, D), jnp.float32), -6.0, 6.0)
    return base.astype(jnp.bfloat16)


def level_of(stream_key, shape, cuts, low, top_value):
    factor_of, own = 1.0, jax.random.fold_in(stream_key, 6)
    for axis_at, parts in cuts:
        heights = jnp.exp(jax.random.uniform(jax.random.fold_in(own, axis_at), (parts,), jnp.float32, low / len(cuts), top_value / len(cuts)))
        factor_of = factor_of * jnp.repeat(heights, shape[axis_at] // parts).reshape([-1 if axis == axis_at else 1 for axis in range(len(shape))])
    return factor_of


def gaussian(own_key, extent, scale, reach, cuts=(), kind=jnp.bfloat16):
    values = scale * jax.random.normal(own_key, extent, jnp.float32)
    if cuts:
        values = values * level_of(own_key, extent, cuts, -0.22, 0.18)
    return jnp.clip(values, -reach, reach).astype(kind)


def setup_inputs(seed: int = 0) -> dict:
    keys = jax.random.split(jax.random.key(seed), 6)
    tokens = draw_tokens(jax.random.fold_in(keys[5], 71), 0)
    cotangent = gaussian(keys[1], (IMAGES, PATCHES, D), 1.0, 6.0, ((0, 256),))
    router = draw_router(jax.random.fold_in(keys[5], 71), 0)
    first_weight = gaussian(keys[3], (EXPERTS, D, EXP_HIDDEN), D ** -0.5, 0.15625, ((0, 64), (2, 4)))
    second_weight = gaussian(keys[4], (EXPERTS, EXP_HIDDEN, D), EXP_HIDDEN ** -0.5, 0.125, ((0, 64), (1, 4)))
    return dict(tokens=tokens, cotangent=cotangent, router=router, first_weight=first_weight, second_weight=second_weight)


ROOT_TWO_OVER_PI = 0.7978845608028654
CUBIC_TERM = 0.044715


def gelu_value(pre_act):
    argument = ROOT_TWO_OVER_PI * (pre_act + CUBIC_TERM * pre_act * pre_act * pre_act)
    return 0.5 * pre_act * (1.0 + jnp.tanh(argument))


def gelu_slope(pre_act):
    argument = ROOT_TWO_OVER_PI * (pre_act + CUBIC_TERM * pre_act * pre_act * pre_act)
    tangent = jnp.tanh(argument)
    return 0.5 * (1.0 + tangent) + 0.5 * pre_act * (1.0 - tangent * tangent) * ROOT_TWO_OVER_PI * (1.0 + 3.0 * CUBIC_TERM * pre_act * pre_act)


def rounded(values):
    return lax.optimization_barrier(values.astype(jnp.bfloat16)).astype(jnp.float32)


def router_probs(image, router):
    logits = jnp.dot(image, router, preferred_element_type=jnp.float32)
    dispatch = jax.nn.softmax(logits, axis=0)
    combine = jax.nn.softmax(logits, axis=1)
    return dispatch, combine


def reference(tokens, cotangent, router, first_weight, second_weight):
    def front(items):
        image, grad_out = items
        dispatch, combine = router_probs(image, router)
        slot_in = jnp.dot(dispatch.astype(jnp.bfloat16).T, image, preferred_element_type=jnp.float32).astype(jnp.bfloat16)
        slot_grad = jnp.dot(combine.astype(jnp.bfloat16).T, grad_out, preferred_element_type=jnp.float32).astype(jnp.bfloat16)
        return slot_in, slot_grad

    slot_in, slot_grad = lax.map(front, (tokens, cotangent))
    block = EXP_HIDDEN // N_DP

    def expert(items):
        rows_in, rows_grad, w_first, w_second = items
        pre_act = jnp.dot(rows_in, w_first, preferred_element_type=jnp.float32)
        hidden_act = gelu_value(pre_act).astype(jnp.bfloat16)
        act_grad = jnp.dot(rows_grad, w_second.T, preferred_element_type=jnp.float32)
        pre_grad = (act_grad * gelu_slope(pre_act)).astype(jnp.bfloat16)
        out_total = jnp.zeros((rows_in.shape[0], D), jnp.float32)
        back_total = jnp.zeros((rows_in.shape[0], D), jnp.float32)
        for part_index in range(N_DP):
            low = part_index * block
            out_total = out_total + rounded(jnp.dot(hidden_act[:, low:low + block], w_second[low:low + block], preferred_element_type=jnp.float32))
            back_total = back_total + rounded(jnp.dot(pre_grad[:, low:low + block], w_first[:, low:low + block].T, preferred_element_type=jnp.float32))
        slot_out = out_total.astype(jnp.bfloat16)
        slot_back = back_total.astype(jnp.bfloat16)
        grad_first = jnp.dot(rows_in.T, pre_grad, preferred_element_type=jnp.float32).astype(jnp.bfloat16)
        grad_second = jnp.dot(hidden_act.T, rows_grad, preferred_element_type=jnp.float32).astype(jnp.bfloat16)
        return slot_out, slot_back, grad_first, grad_second

    slot_out, slot_back, first_grad, second_grad = lax.map(
        expert, (jnp.swapaxes(slot_in, 0, 1), jnp.swapaxes(slot_grad, 0, 1), first_weight, second_weight))
    slot_out = jnp.swapaxes(slot_out, 0, 1)
    slot_back = jnp.swapaxes(slot_back, 0, 1)

    def back(carry, items):
        image, grad_out, out_image, back_image = items
        dispatch, combine = router_probs(image, router)
        combine_grad = jnp.dot(grad_out, out_image.T, preferred_element_type=jnp.float32)
        dispatch_grad = jnp.dot(image, back_image.T, preferred_element_type=jnp.float32)
        logit_grad = dispatch * (dispatch_grad - jnp.sum(dispatch * dispatch_grad, axis=0, keepdims=True))
        logit_grad = logit_grad + combine * (combine_grad - jnp.sum(combine * combine_grad, axis=1, keepdims=True))
        logit_low = logit_grad.astype(jnp.bfloat16)
        token_part = jnp.dot(dispatch.astype(jnp.bfloat16), back_image, preferred_element_type=jnp.float32)
        token_part = token_part + jnp.dot(logit_low, router.T, preferred_element_type=jnp.float32)
        carry = carry + jnp.dot(image.T, logit_low, preferred_element_type=jnp.float32)
        return carry, token_part.astype(jnp.bfloat16)

    router_grad, token_grad = lax.scan(back, jnp.zeros((D, EXPERTS), jnp.float32), (tokens, cotangent, slot_out, slot_back))
    return token_grad, router_grad, first_grad, second_grad
```

```python
import jax
import jax.numpy as jnp
from jax import lax
from jax.sharding import PartitionSpec as P

ROOT_TWO_OVER_PI = 0.7978845608028654
CUBIC_TERM = 0.044715


def gelu_value(pre_act):
    argument = ROOT_TWO_OVER_PI * (pre_act + CUBIC_TERM * pre_act * pre_act * pre_act)
    return 0.5 * pre_act * (1.0 + jnp.tanh(argument))


def gelu_slope(pre_act):
    argument = ROOT_TWO_OVER_PI * (pre_act + CUBIC_TERM * pre_act * pre_act * pre_act)
    tangent = jnp.tanh(argument)
    return 0.5 * (1.0 + tangent) + 0.5 * pre_act * (1.0 - tangent * tangent) * ROOT_TWO_OVER_PI * (
        1.0 + 3.0 * CUBIC_TERM * pre_act * pre_act
    )


def matmul(left, right):
    return jnp.dot(left, right, preferred_element_type=jnp.float32)


def matmul_nt(left, right):
    return lax.dot_general(
        left, right, (((1,), (1,)), ((), ())), preferred_element_type=jnp.float32
    )


def matmul_tn(left, right):
    return lax.dot_general(
        left, right, (((0,), (0,)), ((), ())), preferred_element_type=jnp.float32
    )


def send_grads(slot_grad, model_width):
    arrived = lax.all_to_all(slot_grad, "expert", split_axis=1, concat_axis=0, tiled=True)
    return arrived.reshape(-1, model_width)


def body(tokens, cotangent, router, first_weight, second_weight):
    image_count = tokens.shape[0]
    model_width = tokens.shape[2]
    expert_count = lax.axis_size("expert")
    logits = jnp.einsum("imd,de->ime", tokens, router, preferred_element_type=jnp.float32)
    dispatch = jax.nn.softmax(logits, axis=1)
    combine = jax.nn.softmax(logits, axis=2)
    dispatch_low = dispatch.astype(jnp.bfloat16)
    combine_low = combine.astype(jnp.bfloat16)
    slot_in = jnp.einsum(
        "ime,imd->ied", dispatch_low, tokens, preferred_element_type=jnp.float32
    ).astype(jnp.bfloat16)
    slot_grad = jnp.einsum(
        "ime,imd->ied", combine_low, cotangent, preferred_element_type=jnp.float32
    ).astype(jnp.bfloat16)
    mine_grad = None
    mine_in = lax.all_to_all(slot_in, "expert", split_axis=1, concat_axis=0, tiled=True).reshape(
        -1, model_width
    )
    mine_grad = send_grads(slot_grad, model_width)
    every_in, every_grad = (
        lax.all_gather(mine_in, "dp", axis=0, tiled=True),
        lax.all_gather(mine_grad, "dp", axis=0, tiled=True),
    )
    w_first = first_weight[0]
    w_second = second_weight[0]
    pre_act = matmul(every_in, w_first)
    hidden_act = gelu_value(pre_act).astype(jnp.bfloat16)
    act_grad = matmul_nt(every_grad, w_second)
    pre_grad = (act_grad * gelu_slope(pre_act)).astype(jnp.bfloat16)
    grad_first = matmul_tn(every_in, pre_grad)
    grad_second = matmul_tn(hidden_act, every_grad)
    forward_part = matmul(hidden_act, w_second)
    backward_part = matmul_nt(pre_grad, w_first)
    summed = lax.psum_scatter(
        jnp.concatenate([forward_part, backward_part], axis=1).astype(jnp.bfloat16),
        "dp",
        scatter_dimension=0,
        tiled=True,
    ).astype(jnp.float32)
    slot_out = summed[:, :model_width].astype(jnp.bfloat16)
    slot_back = summed[:, model_width:].astype(jnp.bfloat16)
    shaped_out = slot_out.reshape(expert_count, image_count, 1, model_width)
    shaped_back = slot_back.reshape(expert_count, image_count, 1, model_width)
    back_out, back_grad = (
        lax.all_to_all(shaped_out, "expert", split_axis=0, concat_axis=2, tiled=True),
        lax.all_to_all(shaped_back, "expert", split_axis=0, concat_axis=2, tiled=True),
    )
    expert_out = back_out.reshape(image_count, expert_count, model_width)
    expert_back = back_grad.reshape(image_count, expert_count, model_width)
    combine_grad = jnp.einsum(
        "imd,ied->ime", cotangent, expert_out, preferred_element_type=jnp.float32
    )
    dispatch_grad = jnp.einsum(
        "imd,ied->ime", tokens, expert_back, preferred_element_type=jnp.float32
    )
    logit_grad = dispatch * (
        dispatch_grad - jnp.sum(dispatch * dispatch_grad, axis=1, keepdims=True)
    )
    logit_grad = logit_grad + combine * (
        combine_grad - jnp.sum(combine * combine_grad, axis=2, keepdims=True)
    )
    logit_low = logit_grad.astype(jnp.bfloat16)
    token_part = jnp.einsum(
        "ime,ied->imd", dispatch_low, expert_back, preferred_element_type=jnp.float32
    )
    token_part = token_part + jnp.einsum(
        "ime,de->imd", logit_low, router, preferred_element_type=jnp.float32
    )
    token_grad = token_part.astype(jnp.bfloat16)
    router_part = jnp.einsum("ime,imd->ed", logit_low, tokens, preferred_element_type=jnp.float32)
    router_parts = lax.all_to_all(router_part, "expert", split_axis=0, concat_axis=0, tiled=True)
    router_grad = lax.psum(jnp.sum(router_parts, axis=0), "dp")[:, None]
    return (
        token_grad,
        router_grad,
        grad_first[None].astype(jnp.bfloat16),
        grad_second[None].astype(jnp.bfloat16),
    )


def solution(mesh):
    placed = (
        P(("dp", "expert"), None, None),
        P(("dp", "expert"), None, None),
        P(),
        P("expert", None, "dp"),
        P("expert", "dp", None),
    )
    return jax.shard_map(
        body,
        mesh=mesh,
        in_specs=placed,
        out_specs=(
            P(("dp", "expert"), None, None),
            P(None, "expert"),
            P("expert", None, "dp"),
            P("expert", "dp", None),
        ),
        check_vma=False,
    )
```

```python
import functools

import jax
import jax.numpy as jnp
from jax import lax
from jax.experimental import pallas as pl
from jax.experimental.pallas import tpu as pltpu
from jax.sharding import PartitionSpec as P

ROOT_TWO_OVER_PI = 0.7978845608028654
CUBIC_TERM = 0.044715
MESH = pl.DeviceIdType.MESH
F32, BF16 = jnp.float32, jnp.bfloat16

NZ, NYX = 8, 8
IMG, TOK, DIM, HID, EXP = 2, 256, 1280, 640, 64
CW = 256
NC = DIM // CW
ROWS = 128
N_BLK = 4


def mm(a, b):
    return lax.dot_general(a, b, (((1,), (0,)), ((), ())), preferred_element_type=F32)


def mm_nt(a, b):
    return lax.dot_general(a, b, (((1,), (1,)), ((), ())), preferred_element_type=F32)


def mm_tn(a, b):
    return lax.dot_general(a, b, (((0,), (0,)), ((), ())), preferred_element_type=F32)


def iota(shape, axis):
    return lax.broadcasted_iota(jnp.int32, shape, axis)


def one_hot(mask):
    return jnp.where(mask, 1.0, 0.0).astype(BF16)


def kernel(
    tok_hbm, cot_hbm, rt_hbm, w1_hbm, w2_hbm,
    tg_hbm, rg_out, g1_hbm, g2_hbm,
    tok, cot, rt, w1, w2, ltm, disp, comb, dlow, perm1, perm3,
    send1, recv1, send2, xs, acc_pre, acc_act, hid, pg,
    op, rc, t_own, sx, rx, so, ry, sz, rz, rp, cg, dg, llow,
    tgv, g1v, g2v, rsend, rrecv, rs2, rr2, rs3, rr3, rs4, rr4,
    in_sem, out_sem, z1_sem, y1_sem, agx_sem, agc_sem, agd_sem,
    rc_sem, rx_sem, ry_sem, rz_sem, rt_sem, snd_sem,
):
    p = lax.axis_index("dp")
    q = lax.axis_index("expert")
    z = q % NZ
    yx = q // NZ
    y = yx // 2
    xh = yx % 2

    def z_peer(k):
        zt = (z + k) % NZ
        return zt, (p, yx * NZ + zt)

    def yx_peer(k):
        dx = k % 2
        yt = (y + k // 2) % 4
        yxt = yt * 2 + (xh + dx) % 2
        return yxt, ((p + 2 * dx) % 4, yxt * NZ + z)

    core_peer = (p + 1 - 2 * (p % 2), q)
    x_peer = ((p + 2) % 4, q)

    def remote(src, dst, send_sem, recv_sem, dev):
        pltpu.make_async_remote_copy(
            src_ref=src, dst_ref=dst, send_sem=send_sem, recv_sem=recv_sem,
            device_id=dev, device_id_type=MESH,
        ).start()

    def await_bytes(ref, sem):
        pltpu.make_async_copy(ref, ref, sem).wait()

    def cols(c):
        return pl.ds(pl.multiple_of(c * CW, CW), CW)

    loads = [
        pltpu.make_async_copy(a, b, in_sem.at[i])
        for i, (a, b) in enumerate(
            ((tok_hbm, tok), (rt_hbm, rt), (cot_hbm, cot), (w1_hbm, w1), (w2_hbm, w2))
        )
    ]
    for load in loads:
        load.start()

    barrier = pltpu.get_barrier_semaphore()

    @pl.loop(1, 8)
    def _(k):
        pl.semaphore_signal(barrier, inc=1, device_id=z_peer(k)[1], device_id_type=MESH)
        pl.semaphore_signal(barrier, inc=1, device_id=yx_peer(k)[1], device_id_type=MESH)

    pl.semaphore_signal(barrier, inc=1, device_id=core_peer, device_id_type=MESH)
    pl.semaphore_signal(barrier, inc=1, device_id=x_peer, device_id_type=MESH)

    o1, n1 = iota((256, 256), 0), iota((256, 256), 1)
    perm1[...] = one_hot(
        n1 == ((o1 >> 1) & 7) * 32 + ((o1 >> 4) & 7) * 4 + (o1 >> 7) * 2 + (o1 & 1)
    )
    perm3[...] = one_hot(
        n1 == (o1 & 7) * 32 + ((o1 >> 3) & 7) * 4 + ((o1 >> 6) & 1) * 2 + (o1 >> 7)
    )
    n2, e2 = iota((256, EXP), 0), iota((256, EXP), 1)
    same_slot = e2 == ((n2 >> 2) & 7) * 8 + (n2 >> 5)

    loads[0].wait()
    loads[1].wait()
    logits = mm(tok[...], rt[...])
    for i in range(IMG):
        rows = pl.ds(i * TOK, TOK)
        part = logits[i * TOK:(i + 1) * TOK]
        up = jnp.exp(part - jnp.max(part, axis=0, keepdims=True))
        d = up / jnp.sum(up, axis=0, keepdims=True)
        up = jnp.exp(part - jnp.max(part, axis=1, keepdims=True))
        c = up / jnp.sum(up, axis=1, keepdims=True)
        disp[rows, :] = d
        comb[rows, :] = c
        d_low = d.astype(BF16)
        dlow[rows, :] = d_low
        for a, low in ((0, d_low), (1, c.astype(BF16))):
            spread = one_hot(same_slot & ((n2 & 3) == a * 2 + i))
            ltm[:, pl.ds(a * 512 + i * TOK, TOK)] = mm_nt(spread, low).astype(BF16)
    loads[2].wait()
    pl.semaphore_wait(barrier, 16)

    def send_slots(c):
        ch = cols(c)
        send1[:, ch] = (
            mm(ltm[:, :512], tok[:, ch]) + mm(ltm[:, 512:], cot[:, ch])
        ).astype(BF16)
        mine = pl.ds(pl.multiple_of(z * 32, 32), 32)
        pltpu.make_async_copy(send1.at[mine, ch], recv1.at[mine, ch], z1_sem.at[c]).start()

        @pl.loop(1, 8)
        def _(k):
            zt, dev = z_peer(k)
            remote(
                send1.at[pl.ds(pl.multiple_of(zt * 32, 32), 32), ch], recv1.at[mine, ch],
                snd_sem.at[0], z1_sem.at[c], dev,
            )

    def turn_slots(c):
        ch = cols(c)
        await_bytes(recv1.at[:, ch], z1_sem.at[c])
        send2[:, :, ch] = mm(perm1[...], recv1[:, ch]).astype(BF16).reshape(2, ROWS, CW)
        mine = pl.ds(pl.multiple_of(yx * 16, 16), 16)
        pltpu.make_async_copy(
            send2.at[:, mine, ch], xs.at[0, :, mine, ch], y1_sem.at[c]
        ).start()

        @pl.loop(1, 8)
        def _(k):
            yxt, dev = yx_peer(k)
            remote(
                send2.at[:, pl.ds(pl.multiple_of(yxt * 16, 16), 16), ch],
                xs.at[0, :, mine, ch], snd_sem.at[1], y1_sem.at[c], dev,
            )

    def gather_slots(c):
        ch = cols(c)
        await_bytes(xs.at[0, :, :, ch], y1_sem.at[c])
        remote(xs.at[0, :, :, ch], xs.at[1, :, :, ch], snd_sem.at[2], agx_sem.at[c], x_peer)
        remote(xs.at[0, :, :, ch], xs.at[2, :, :, ch], snd_sem.at[3], agc_sem.at[c], core_peer)

    def forward_slots(c):
        ch = cols(c)
        await_bytes(xs.at[1, :, :, ch], agx_sem.at[c])
        remote(xs.at[1, :, :, ch], xs.at[3, :, :, ch], snd_sem.at[4], agd_sem.at[c], core_peer)

    acc_pre[...] = jnp.zeros_like(acc_pre)
    acc_act[...] = jnp.zeros_like(acc_act)

    def first_layer(c):
        ch = cols(c)
        await_bytes(xs.at[2, :, :, ch], agc_sem.at[c])
        await_bytes(xs.at[3, :, :, ch], agd_sem.at[c])
        acc_pre[...] += mm(xs[:, 0, :, ch].reshape(N_BLK * ROWS, CW), w1[ch, :])
        acc_act[...] += mm_nt(xs[:, 1, :, ch].reshape(N_BLK * ROWS, CW), w2[:, ch])

    def staged(step, stages):
        for lag, stage in stages:
            @pl.when((step >= lag) & (step < lag + NC))
            def _(stage=stage, lag=lag):
                stage(step - lag)

    loads[3].wait()
    loads[4].wait()

    @pl.loop(0, NC + 5)
    def _(step):
        staged(step, (
            (0, send_slots), (2, turn_slots), (3, gather_slots), (4, forward_slots),
            (5, first_layer),
        ))

    @pl.loop(0, 8)
    def _(b):
        rows = pl.ds(pl.multiple_of(b * 64, 64), 64)
        u = acc_pre[rows, :]
        square = u * u
        tangent = jnp.tanh(ROOT_TWO_OVER_PI * (u + CUBIC_TERM * square * u))
        hid[rows, :] = (0.5 * u * (1.0 + tangent)).astype(BF16)
        slope = 0.5 * (1.0 + tangent) + 0.5 * u * (1.0 - tangent * tangent) * ROOT_TWO_OVER_PI * (
            1.0 + 3.0 * CUBIC_TERM * square
        )
        pg[rows, :] = (acc_act[rows, :] * slope).astype(BF16)

    cg[...] = jnp.zeros_like(cg)
    dg[...] = jnp.zeros_like(dg)

    def second_layer(c):
        ch = cols(c)
        op[:, 0, :, ch] = mm(hid[...], w2[:, ch]).astype(BF16).reshape(N_BLK, ROWS, CW)
        op[:, 1, :, ch] = mm_nt(pg[...], w1[ch, :]).astype(BF16).reshape(N_BLK, ROWS, CW)
        remote(
            op.at[pl.ds(2, 2), :, :, ch], rc.at[:, :, :, ch], snd_sem.at[5], rc_sem.at[c], core_peer
        )

    def core_sum(c):
        ch = cols(c)
        await_bytes(rc.at[:, :, :, ch], rc_sem.at[c])
        sx[:, :, ch] = (op[1, :, :, ch].astype(F32) + rc[1, :, :, ch].astype(F32)).astype(BF16)
        remote(sx.at[:, :, ch], rx.at[:, :, ch], snd_sem.at[6], rx_sem.at[c], x_peer)
        t_own[:, :, ch] = op[0, :, :, ch].astype(F32) + rc[0, :, :, ch].astype(F32)

    def weight_grads(c):
        ch = cols(c)
        g1v[ch, :] = mm_tn(xs[:, 0, :, ch].reshape(N_BLK * ROWS, CW), pg[...]).astype(BF16)
        g2v[:, ch] = mm_tn(hid[...], xs[:, 1, :, ch].reshape(N_BLK * ROWS, CW)).astype(BF16)

    def x_sum(c):
        ch = cols(c)
        await_bytes(rx.at[:, :, ch], rx_sem.at[c])
        so[:, :, ch] = (t_own[:, :, ch] + rx[:, :, ch].astype(F32)).astype(BF16)
        mine = pl.ds(pl.multiple_of(yx * 16, 16), 16)
        pltpu.make_async_copy(so.at[:, mine, ch], ry.at[:, mine, ch], ry_sem.at[c]).start()

        @pl.loop(1, 8)
        def _(k):
            yxt, dev = yx_peer(k)
            remote(
                so.at[:, pl.ds(pl.multiple_of(yxt * 16, 16), 16), ch],
                ry.at[:, mine, ch], snd_sem.at[7], ry_sem.at[c], dev,
            )

    def turn_back(c):
        ch = cols(c)
        await_bytes(ry.at[:, :, ch], ry_sem.at[c])
        sz[:, ch] = mm_tn(perm1[...], ry[:, :, ch].reshape(2 * ROWS, CW)).astype(BF16)
        mine = pl.ds(pl.multiple_of(z * 32, 32), 32)
        pltpu.make_async_copy(sz.at[mine, ch], rz.at[mine, ch], rz_sem.at[c]).start()

        @pl.loop(1, 8)
        def _(k):
            zt, dev = z_peer(k)
            remote(
                sz.at[pl.ds(pl.multiple_of(zt * 32, 32), 32), ch], rz.at[mine, ch],
                snd_sem.at[8], rz_sem.at[c], dev,
            )

    def slots_back(c):
        ch = cols(c)
        await_bytes(rz.at[:, ch], rz_sem.at[c])
        rp[:, ch] = mm(perm3[...], rz[:, ch]).astype(BF16)
        for i in range(IMG):
            rows = pl.ds(i * TOK, TOK)
            cg[rows, :] += mm_nt(cot[rows, ch], rp[pl.ds(i * 128, EXP), ch])
            dg[rows, :] += mm_nt(tok[rows, ch], rp[pl.ds(i * 128 + EXP, EXP), ch])

    @pl.loop(0, NC + 6)
    def _(step):
        staged(step, (
            (0, second_layer), (1, core_sum), (1, weight_grads), (2, x_sum), (4, turn_back),
            (6, slots_back),
        ))

    stores = [
        pltpu.make_async_copy(g1v, g1_hbm, out_sem.at[0]),
        pltpu.make_async_copy(g2v, g2_hbm, out_sem.at[1]),
    ]
    for store in stores:
        store.start()

    for i in range(IMG):
        rows = pl.ds(i * TOK, TOK)
        d, c = disp[rows, :], comb[rows, :]
        d_grad, c_grad = dg[rows, :], cg[rows, :]
        grad = d * (d_grad - jnp.sum(d * d_grad, axis=0, keepdims=True))
        grad = grad + c * (c_grad - jnp.sum(c * c_grad, axis=1, keepdims=True))
        llow[rows, :] = grad.astype(BF16)

    e3, j3 = iota((EXP, EXP), 0), iota((EXP, EXP), 1)
    by_z = one_hot(e3 == (j3 & 7) * 8 + (j3 >> 3))
    turned = mm(llow[...], by_z).astype(BF16)
    part = mm_tn(turned, tok[...])
    for k in range(NZ):
        rows = part[k * 8:(k + 1) * 8]
        rsend[pl.ds(k * 16, 16), :] = jnp.concatenate(
            [rows[:, :HID], rows[:, HID:]], axis=0
        ).astype(BF16)
    mine_z = pl.ds(pl.multiple_of(z * 16, 16), 16)
    pltpu.make_async_copy(rsend.at[mine_z], rrecv.at[mine_z], rt_sem.at[0]).start()

    @pl.loop(1, 8)
    def _(k):
        zt, dev = z_peer(k)
        remote(
            rsend.at[pl.ds(pl.multiple_of(zt * 16, 16), 16)], rrecv.at[mine_z],
            snd_sem.at[9], rt_sem.at[0], dev,
        )

    for i in range(IMG):
        rows = pl.ds(i * TOK, TOK)

        @pl.loop(0, NC)
        def _(c, i=i, rows=rows):
            ch = cols(c)
            tgv[rows, ch] = (
                mm(dlow[rows, :], rp[pl.ds(i * 128 + EXP, EXP), ch]) + mm_nt(llow[rows, :], rt[ch, :])
            ).astype(BF16)

    stores.append(pltpu.make_async_copy(tgv, tg_hbm, out_sem.at[2]))
    stores[2].start()

    await_bytes(rrecv, rt_sem.at[0])
    total = rrecv[pl.ds(0, 16), :].astype(F32)
    for k in range(1, NZ):
        total = total + rrecv[pl.ds(k * 16, 16), :].astype(F32)
    for k in range(NYX):
        rs2[k, pl.ds(0, 1), :] = total[k:k + 1]
        rs2[k, pl.ds(1, 1), :] = total[8 + k:9 + k]
    pltpu.make_async_copy(rs2.at[yx], rr2.at[yx], rt_sem.at[1]).start()

    @pl.loop(1, 8)
    def _(k):
        yxt, dev = yx_peer(k)
        remote(rs2.at[yxt], rr2.at[yx], snd_sem.at[10], rt_sem.at[1], dev)

    await_bytes(rr2, rt_sem.at[1])
    rs3[...] = jnp.sum(rr2[...], axis=0)
    remote(rs3, rr3, snd_sem.at[11], rt_sem.at[2], x_peer)
    await_bytes(rr3, rt_sem.at[2])
    rs4[...] = rs3[...] + rr3[...]
    remote(rs4, rr4, snd_sem.at[12], rt_sem.at[3], core_peer)
    await_bytes(rr4, rt_sem.at[3])
    rg_out[...] = rs4[...] + rr4[...]

    for store in stores:
        store.wait()
    for ref, number in (
        (send1.at[pl.ds(0, 224)], 0), (send2.at[:, pl.ds(0, 112)], 1),
        (xs.at[0], 2), (xs.at[0], 3), (xs.at[1], 4), (rc, 5), (sx, 6),
        (so.at[:, pl.ds(0, 112)], 7), (sz.at[pl.ds(0, 224)], 8),
        (rsend.at[pl.ds(0, 112)], 9), (rs2.at[pl.ds(0, 7)], 10), (rs3, 11), (rs4, 12),
    ):
        await_bytes(ref, snd_sem.at[number])


def body(tokens, cotangent, router, first_weight, second_weight):
    vmem, dma = pltpu.VMEM, pltpu.SemaphoreType.DMA
    token_grad, router_column, first_grad, second_grad = pl.pallas_call(
        kernel,
        out_shape=(
            jax.ShapeDtypeStruct((IMG * TOK, DIM), BF16),
            jax.ShapeDtypeStruct((2, HID), F32),
            jax.ShapeDtypeStruct((DIM, HID), BF16),
            jax.ShapeDtypeStruct((HID, DIM), BF16),
        ),
        in_specs=[pl.BlockSpec(memory_space=pl.ANY)] * 5,
        out_specs=(
            pl.BlockSpec(memory_space=pl.ANY),
            pl.BlockSpec(memory_space=pltpu.VMEM),
            pl.BlockSpec(memory_space=pl.ANY),
            pl.BlockSpec(memory_space=pl.ANY),
        ),
        scratch_shapes=[
            vmem((IMG * TOK, DIM), BF16),
            vmem((IMG * TOK, DIM), BF16),
            vmem((DIM, EXP), BF16),
            vmem((DIM, HID), BF16),
            vmem((HID, DIM), BF16),
            vmem((256, 1024), BF16),
            vmem((IMG * TOK, EXP), F32),
            vmem((IMG * TOK, EXP), F32),
            vmem((IMG * TOK, EXP), BF16),
            vmem((256, 256), BF16),
            vmem((256, 256), BF16),
            vmem((256, DIM), BF16),
            vmem((256, DIM), BF16),
            vmem((2, ROWS, DIM), BF16),
            vmem((N_BLK, 2, ROWS, DIM), BF16),
            vmem((N_BLK * ROWS, HID), F32),
            vmem((N_BLK * ROWS, HID), F32),
            vmem((N_BLK * ROWS, HID), BF16),
            vmem((N_BLK * ROWS, HID), BF16),
            vmem((N_BLK, 2, ROWS, DIM), BF16),
            vmem((2, 2, ROWS, DIM), BF16),
            vmem((2, ROWS, DIM), F32),
            vmem((2, ROWS, DIM), BF16),
            vmem((2, ROWS, DIM), BF16),
            vmem((2, ROWS, DIM), BF16),
            vmem((2, ROWS, DIM), BF16),
            vmem((256, DIM), BF16),
            vmem((256, DIM), BF16),
            vmem((256, DIM), BF16),
            vmem((IMG * TOK, EXP), F32),
            vmem((IMG * TOK, EXP), F32),
            vmem((IMG * TOK, EXP), BF16),
            vmem((IMG * TOK, DIM), BF16),
            vmem((DIM, HID), BF16),
            vmem((HID, DIM), BF16),
            vmem((NZ * 16, HID), BF16),
            vmem((NZ * 16, HID), BF16),
            vmem((NYX, 2, HID), F32),
            vmem((NYX, 2, HID), F32),
            vmem((2, HID), F32),
            vmem((2, HID), F32),
            vmem((2, HID), F32),
            vmem((2, HID), F32),
            dma((5,)), dma((3,)),
            dma((NC,)), dma((NC,)), dma((NC,)), dma((NC,)), dma((NC,)),
            dma((NC,)), dma((NC,)), dma((NC,)), dma((NC,)),
            dma((4,)), dma((13,)),
        ],
        compiler_params=pltpu.CompilerParams(
            collective_id=0, has_side_effects=True, vmem_limit_bytes=56 * 1024 * 1024
        ),
    )(
        tokens.reshape(IMG * TOK, DIM), cotangent.reshape(IMG * TOK, DIM), router,
        first_weight[0], second_weight[0],
    )
    return (
        token_grad.reshape(IMG, TOK, DIM),
        router_column.reshape(DIM, 1),
        first_grad[None],
        second_grad[None],
    )


def solution(mesh):
    placed = (
        P(("dp", "expert"), None, None),
        P(("dp", "expert"), None, None),
        P(),
        P("expert", None, "dp"),
        P("expert", "dp", None),
    )
    return jax.shard_map(
        body,
        mesh=mesh,
        in_specs=placed,
        out_specs=(
            P(("dp", "expert"), None, None),
            P(None, "expert"),
            P("expert", None, "dp"),
            P("expert", "dp", None),
        ),
        check_vma=False,
    )
```

```python
import functools

import jax
import jax.numpy as jnp
from jax import lax
from jax.experimental import pallas as pl
from jax.experimental.pallas import tpu as pltpu
from jax.sharding import PartitionSpec as P

ROOT_TWO_OVER_PI = 0.7978845608028654
CUBIC_TERM = 0.044715
MESH = pl.DeviceIdType.MESH
F32, BF16 = jnp.float32, jnp.bfloat16

NZ, NYX = 8, 8
IMG, TOK, DIM, HID, EXP = 2, 256, 1280, 640, 64
CW = 256
NC = DIM // CW
ROWS = 128
N_BLK = 4


def mm(a, b):
    return lax.dot_general(a, b, (((1,), (0,)), ((), ())), preferred_element_type=F32)


def mm_nt(a, b):
    return lax.dot_general(a, b, (((1,), (1,)), ((), ())), preferred_element_type=F32)


def mm_tn(a, b):
    return lax.dot_general(a, b, (((0,), (0,)), ((), ())), preferred_element_type=F32)


def iota(shape, axis):
    return lax.broadcasted_iota(jnp.int32, shape, axis)


def one_hot(mask):
    return jnp.where(mask, 1.0, 0.0).astype(BF16)


def kernel(
    tok_hbm, cot_hbm, rt_hbm, w1_hbm, w2_hbm,
    tgv, rg_out, g1v, g2v,
    tok, cot, rt, w1, w2, ltm, disp, comb, dlow, perm1, perm3,
    send1, recv1, send2, xs, acc_pre, acc_act, hid, pg,
    op, rc, t_own, sx, rx, so, ry, sz, rz, rp, cg, dg, llow,
    rsend, rrecv, rs2, rr2, rs3, rr3,
    in_sem, z1_sem, y1_sem, agx_sem, agc_sem, agd_sem,
    rc_sem, rx_sem, ry_sem, rz_sem, rt_sem, snd_sem,
):
    p = lax.axis_index("dp")
    q = lax.axis_index("expert")
    z = q % NZ
    yx = q // NZ
    y = yx // 2
    xh = yx % 2

    def z_peer(k):
        zt = (z + (k + 1) // 2 * (2 * (k % 2) - 1) + NZ) % NZ
        return zt, (p, yx * NZ + zt)

    def yx_peer(k):
        dx = k % 2
        yt = (y + k // 2) % 4
        yxt = yt * 2 + (xh + dx) % 2
        return yxt, ((p + 2 * dx) % 4, yxt * NZ + z)

    core_peer = (p + 1 - 2 * (p % 2), q)
    x_peer = ((p + 2) % 4, q)

    def remote(src, dst, send_sem, recv_sem, dev):
        pltpu.make_async_remote_copy(
            src_ref=src, dst_ref=dst, send_sem=send_sem, recv_sem=recv_sem,
            device_id=dev, device_id_type=MESH,
        ).start()

    def await_bytes(ref, sem):
        pltpu.make_async_copy(ref, ref, sem).wait()

    def cols(c):
        return pl.ds(pl.multiple_of(c * CW, CW), CW)

    loads = [
        pltpu.make_async_copy(a, b, in_sem.at[i])
        for i, (a, b) in enumerate(
            ((tok_hbm, tok), (rt_hbm, rt), (cot_hbm, cot), (w1_hbm, w1), (w2_hbm, w2))
        )
    ]
    for load in loads:
        load.start()

    barrier = pltpu.get_barrier_semaphore()

    @pl.loop(1, 8)
    def _(k):
        pl.semaphore_signal(barrier, inc=1, device_id=z_peer(k)[1], device_id_type=MESH)
        pl.semaphore_signal(barrier, inc=1, device_id=yx_peer(k)[1], device_id_type=MESH)

    for k in range(1, 4):
        pl.semaphore_signal(barrier, inc=1, device_id=((p + k) % 4, q), device_id_type=MESH)

    o1, n1 = iota((256, 256), 0), iota((256, 256), 1)
    perm1[...] = one_hot(
        n1 == ((o1 >> 1) & 7) * 32 + ((o1 >> 4) & 7) * 4 + (o1 >> 7) * 2 + (o1 & 1)
    )
    perm3[...] = one_hot(
        n1 == (o1 & 7) * 32 + ((o1 >> 3) & 7) * 4 + ((o1 >> 6) & 1) * 2 + (o1 >> 7)
    )
    n2, e2 = iota((256, EXP), 0), iota((256, EXP), 1)
    same_slot = e2 == ((n2 >> 2) & 7) * 8 + (n2 >> 5)

    loads[0].wait()
    loads[1].wait()
    logits = mm_nt(tok[...], rt[...])
    for i in range(IMG):
        rows = pl.ds(i * TOK, TOK)
        part = logits[i * TOK:(i + 1) * TOK]
        up = jnp.exp(part - jnp.max(part, axis=0, keepdims=True))
        d = up / jnp.sum(up, axis=0, keepdims=True)
        up = jnp.exp(part - jnp.max(part, axis=1, keepdims=True))
        c = up / jnp.sum(up, axis=1, keepdims=True)
        disp[rows, :] = d
        comb[rows, :] = c
        d_low = d.astype(BF16)
        dlow[rows, :] = d_low
        for a, low in ((0, d_low), (1, c.astype(BF16))):
            spread = one_hot(same_slot & ((n2 & 3) == a * 2 + i))
            ltm[:, pl.ds(a * 512 + i * TOK, TOK)] = mm_nt(spread, low).astype(BF16)
    loads[2].wait()
    pl.semaphore_wait(barrier, 17)

    def send_slots(c):
        ch = cols(c)
        send1[:, ch] = (
            mm(ltm[:, :512], tok[:, ch]) + mm(ltm[:, 512:], cot[:, ch])
        ).astype(BF16)
        mine = pl.ds(pl.multiple_of(z * 32, 32), 32)
        pltpu.make_async_copy(send1.at[mine, ch], recv1.at[mine, ch], z1_sem.at[c]).start()

        @pl.loop(1, 8)
        def _(k):
            zt, dev = z_peer(k)
            remote(
                send1.at[pl.ds(pl.multiple_of(zt * 32, 32), 32), ch], recv1.at[mine, ch],
                snd_sem.at[0], z1_sem.at[c], dev,
            )

    def turn_slots(c):
        ch = cols(c)
        await_bytes(recv1.at[:, ch], z1_sem.at[c])
        send2[:, :, ch] = mm(perm1[...], recv1[:, ch]).astype(BF16).reshape(2, ROWS, CW)
        mine = pl.ds(pl.multiple_of(yx * 16, 16), 16)
        pltpu.make_async_copy(
            send2.at[:, mine, ch], xs.at[0, :, mine, ch], y1_sem.at[c]
        ).start()

        @pl.loop(1, 8)
        def _(k):
            yxt, dev = yx_peer(k)
            remote(
                send2.at[:, pl.ds(pl.multiple_of(yxt * 16, 16), 16), ch],
                xs.at[0, :, mine, ch], snd_sem.at[1], y1_sem.at[c], dev,
            )

    def gather_slots(c):
        ch = cols(c)
        await_bytes(xs.at[0, :, :, ch], y1_sem.at[c])
        remote(xs.at[0, :, :, ch], xs.at[1, :, :, ch], snd_sem.at[2], agx_sem.at[c], x_peer)
        remote(xs.at[0, :, :, ch], xs.at[2, :, :, ch], snd_sem.at[3], agc_sem.at[c], core_peer)

    def forward_slots(c):
        ch = cols(c)
        await_bytes(xs.at[1, :, :, ch], agx_sem.at[c])
        remote(xs.at[1, :, :, ch], xs.at[3, :, :, ch], snd_sem.at[4], agd_sem.at[c], core_peer)

    acc_pre[...] = jnp.zeros_like(acc_pre)
    acc_act[...] = jnp.zeros_like(acc_act)

    def first_layer(c):
        ch = cols(c)
        await_bytes(xs.at[2, :, :, ch], agc_sem.at[c])
        await_bytes(xs.at[3, :, :, ch], agd_sem.at[c])
        acc_pre[...] += mm(xs[:, 0, :, ch].reshape(N_BLK * ROWS, CW), w1[ch, :])
        acc_act[...] += mm_nt(xs[:, 1, :, ch].reshape(N_BLK * ROWS, CW), w2[:, ch])

    def staged(step, stages):
        for lag, stage in stages:
            @pl.when((step >= lag) & (step < lag + NC))
            def _(stage=stage, lag=lag):
                stage(step - lag)

    loads[3].wait()
    loads[4].wait()

    @pl.loop(0, NC + 5)
    def _(step):
        staged(step, (
            (0, send_slots), (2, turn_slots), (3, gather_slots), (4, forward_slots),
            (5, first_layer),
        ))

    @pl.loop(0, 8)
    def _(b):
        rows = pl.ds(pl.multiple_of(b * 64, 64), 64)
        u = acc_pre[rows, :]
        square = u * u
        tangent = jnp.tanh(ROOT_TWO_OVER_PI * (u + CUBIC_TERM * square * u))
        hid[rows, :] = (0.5 * u * (1.0 + tangent)).astype(BF16)
        slope = 0.5 * (1.0 + tangent) + 0.5 * u * (1.0 - tangent * tangent) * ROOT_TWO_OVER_PI * (
            1.0 + 3.0 * CUBIC_TERM * square
        )
        pg[rows, :] = (acc_act[rows, :] * slope).astype(BF16)

    cg[...] = jnp.zeros_like(cg)
    dg[...] = jnp.zeros_like(dg)

    def second_layer(c):
        ch = cols(c)
        op[:, 0, :, ch] = mm(hid[...], w2[:, ch]).astype(BF16).reshape(N_BLK, ROWS, CW)
        op[:, 1, :, ch] = mm_nt(pg[...], w1[ch, :]).astype(BF16).reshape(N_BLK, ROWS, CW)
        remote(
            op.at[pl.ds(2, 2), :, :, ch], rc.at[:, :, :, ch], snd_sem.at[5], rc_sem.at[c], core_peer
        )

    def core_sum(c):
        ch = cols(c)
        await_bytes(rc.at[:, :, :, ch], rc_sem.at[c])
        sx[:, :, ch] = (op[1, :, :, ch].astype(F32) + rc[1, :, :, ch].astype(F32)).astype(BF16)
        remote(sx.at[:, :, ch], rx.at[:, :, ch], snd_sem.at[6], rx_sem.at[c], x_peer)
        t_own[:, :, ch] = op[0, :, :, ch].astype(F32) + rc[0, :, :, ch].astype(F32)

    def weight_grads(c):
        ch = cols(c)
        g1v[ch, :] = mm_tn(xs[:, 0, :, ch].reshape(N_BLK * ROWS, CW), pg[...]).astype(BF16)
        g2v[:, ch] = mm_tn(hid[...], xs[:, 1, :, ch].reshape(N_BLK * ROWS, CW)).astype(BF16)

    def x_sum(c):
        ch = cols(c)
        await_bytes(rx.at[:, :, ch], rx_sem.at[c])
        so[:, :, ch] = (t_own[:, :, ch] + rx[:, :, ch].astype(F32)).astype(BF16)
        mine = pl.ds(pl.multiple_of(yx * 16, 16), 16)
        pltpu.make_async_copy(so.at[:, mine, ch], ry.at[:, mine, ch], ry_sem.at[c]).start()

        @pl.loop(1, 8)
        def _(k):
            yxt, dev = yx_peer(k)
            remote(
                so.at[:, pl.ds(pl.multiple_of(yxt * 16, 16), 16), ch],
                ry.at[:, mine, ch], snd_sem.at[7], ry_sem.at[c], dev,
            )

    def turn_back(c):
        ch = cols(c)
        await_bytes(ry.at[:, :, ch], ry_sem.at[c])
        sz[:, ch] = mm_tn(perm1[...], ry[:, :, ch].reshape(2 * ROWS, CW)).astype(BF16)
        mine = pl.ds(pl.multiple_of(z * 32, 32), 32)
        pltpu.make_async_copy(sz.at[mine, ch], rz.at[mine, ch], rz_sem.at[c]).start()

        @pl.loop(1, 8)
        def _(k):
            zt, dev = z_peer(k)
            remote(
                sz.at[pl.ds(pl.multiple_of(zt * 32, 32), 32), ch], rz.at[mine, ch],
                snd_sem.at[8], rz_sem.at[c], dev,
            )

    def slots_back(c):
        ch = cols(c)
        await_bytes(rz.at[:, ch], rz_sem.at[c])
        rp[:, ch] = mm(perm3[...], rz[:, ch]).astype(BF16)
        for i in range(IMG):
            rows = pl.ds(i * TOK, TOK)
            cg[rows, :] += mm_nt(cot[rows, ch], rp[pl.ds(i * 128, EXP), ch])
            dg[rows, :] += mm_nt(tok[rows, ch], rp[pl.ds(i * 128 + EXP, EXP), ch])

    @pl.loop(0, NC + 6)
    def _(step):
        staged(step, (
            (0, second_layer), (1, core_sum), (1, weight_grads), (2, x_sum), (4, turn_back),
            (6, slots_back),
        ))

    for i in range(IMG):
        rows = pl.ds(i * TOK, TOK)
        d, c = disp[rows, :], comb[rows, :]
        d_grad, c_grad = dg[rows, :], cg[rows, :]
        grad = d * (d_grad - jnp.sum(d * d_grad, axis=0, keepdims=True))
        grad = grad + c * (c_grad - jnp.sum(c * c_grad, axis=1, keepdims=True))
        llow[rows, :] = grad.astype(BF16)

    e3, j3 = iota((EXP, EXP), 0), iota((EXP, EXP), 1)
    by_z = one_hot(e3 == (j3 & 7) * 8 + (j3 >> 3))
    turned = mm(llow[...], by_z).astype(BF16)
    part = mm_tn(turned, tok[...])
    for k in range(NZ):
        rows = part[k * 8:(k + 1) * 8]
        rsend[pl.ds(k * 16, 16), :] = jnp.concatenate(
            [rows[:, :HID], rows[:, HID:]], axis=0
        ).astype(BF16)
    mine_z = pl.ds(pl.multiple_of(z * 16, 16), 16)
    pltpu.make_async_copy(rsend.at[mine_z], rrecv.at[mine_z], rt_sem.at[0]).start()

    @pl.loop(1, 8)
    def _(k):
        zt, dev = z_peer(k)
        remote(
            rsend.at[pl.ds(pl.multiple_of(zt * 16, 16), 16)], rrecv.at[mine_z],
            snd_sem.at[9], rt_sem.at[0], dev,
        )

    for i in range(IMG):
        rows = pl.ds(i * TOK, TOK)

        @pl.loop(0, NC)
        def _(c, i=i, rows=rows):
            ch = cols(c)
            tgv[rows, ch] = (
                mm(dlow[rows, :], rp[pl.ds(i * 128 + EXP, EXP), ch]) + mm(llow[rows, :], rt[:, ch])
            ).astype(BF16)

    await_bytes(rrecv, rt_sem.at[0])
    total = rrecv[pl.ds(0, 16), :].astype(F32)
    for k in range(1, NZ):
        total = total + rrecv[pl.ds(k * 16, 16), :].astype(F32)
    for k in range(NYX):
        rs2[k, pl.ds(0, 1), :] = total[k:k + 1]
        rs2[k, pl.ds(1, 1), :] = total[8 + k:9 + k]
    pltpu.make_async_copy(rs2.at[yx], rr2.at[yx], rt_sem.at[1]).start()

    @pl.loop(1, 8)
    def _(k):
        yxt, dev = yx_peer(k)
        remote(rs2.at[yxt], rr2.at[yx], snd_sem.at[10], rt_sem.at[1], dev)

    await_bytes(rr2, rt_sem.at[1])
    rs3[...] = jnp.sum(rr2[...], axis=0)
    pltpu.make_async_copy(rs3, rr3.at[p], rt_sem.at[2]).start()
    for k in range(1, 4):
        remote(rs3, rr3.at[p], snd_sem.at[11], rt_sem.at[2], ((p + k) % 4, q))
    await_bytes(rr3, rt_sem.at[2])
    rg_out[...] = (rr3[0] + rr3[1]) + (rr3[2] + rr3[3])

    for ref, number in (
        (send1.at[pl.ds(0, 224)], 0), (send2.at[:, pl.ds(0, 112)], 1),
        (xs.at[0], 2), (xs.at[0], 3), (xs.at[1], 4), (rc, 5), (sx, 6),
        (so.at[:, pl.ds(0, 112)], 7), (sz.at[pl.ds(0, 224)], 8),
        (rsend.at[pl.ds(0, 112)], 9), (rs2.at[pl.ds(0, 7)], 10), (rr3.at[pl.ds(0, 3)], 11),
    ):
        await_bytes(ref, snd_sem.at[number])


def store_kernel(tg, rg, g1, g2, tg_hbm, rg_out, g1_hbm, g2_hbm, sem):
    stores = [
        pltpu.make_async_copy(a, b, sem.at[i])
        for i, (a, b) in enumerate(((g1, g1_hbm), (g2, g2_hbm), (tg, tg_hbm)))
    ]
    for store in stores:
        store.start()
    rg_out[:, :HID] = rg[0:1, :]
    rg_out[:, HID:] = rg[1:2, :]
    for store in stores:
        store.wait()


def body(tokens, cotangent, router, first_weight, second_weight):
    vmem, dma = pltpu.VMEM, pltpu.SemaphoreType.DMA
    results = pl.pallas_call(
        kernel,
        out_shape=(
            vmem((IMG * TOK, DIM), BF16),
            vmem((2, HID), F32),
            vmem((DIM, HID), BF16),
            vmem((HID, DIM), BF16),
        ),
        in_specs=[pl.BlockSpec(memory_space=pltpu.HBM)] * 5,
        out_specs=(pl.BlockSpec(memory_space=pltpu.VMEM),) * 4,
        scratch_shapes=[
            vmem((IMG * TOK, DIM), BF16),
            vmem((IMG * TOK, DIM), BF16),
            vmem((EXP, DIM), BF16),
            vmem((DIM, HID), BF16),
            vmem((HID, DIM), BF16),
            vmem((256, 1024), BF16),
            vmem((IMG * TOK, EXP), F32),
            vmem((IMG * TOK, EXP), F32),
            vmem((IMG * TOK, EXP), BF16),
            vmem((256, 256), BF16),
            vmem((256, 256), BF16),
            vmem((256, DIM), BF16),
            vmem((256, DIM), BF16),
            vmem((2, ROWS, DIM), BF16),
            vmem((N_BLK, 2, ROWS, DIM), BF16),
            vmem((N_BLK * ROWS, HID), F32),
            vmem((N_BLK * ROWS, HID), F32),
            vmem((N_BLK * ROWS, HID), BF16),
            vmem((N_BLK * ROWS, HID), BF16),
            vmem((N_BLK, 2, ROWS, DIM), BF16),
            vmem((2, 2, ROWS, DIM), BF16),
            vmem((2, ROWS, DIM), F32),
            vmem((2, ROWS, DIM), BF16),
            vmem((2, ROWS, DIM), BF16),
            vmem((2, ROWS, DIM), BF16),
            vmem((2, ROWS, DIM), BF16),
            vmem((256, DIM), BF16),
            vmem((256, DIM), BF16),
            vmem((256, DIM), BF16),
            vmem((IMG * TOK, EXP), F32),
            vmem((IMG * TOK, EXP), F32),
            vmem((IMG * TOK, EXP), BF16),
            vmem((NZ * 16, HID), BF16),
            vmem((NZ * 16, HID), BF16),
            vmem((NYX, 2, HID), F32),
            vmem((NYX, 2, HID), F32),
            vmem((2, HID), F32),
            vmem((4, 2, HID), F32),
            dma((5,)),
            dma((NC,)), dma((NC,)), dma((NC,)), dma((NC,)), dma((NC,)),
            dma((NC,)), dma((NC,)), dma((NC,)), dma((NC,)),
            dma((3,)), dma((12,)),
        ],
        compiler_params=pltpu.CompilerParams(
            collective_id=0, has_side_effects=True, vmem_limit_bytes=56 * 1024 * 1024
        ),
    )(
        tokens.reshape(IMG * TOK, DIM), cotangent.reshape(IMG * TOK, DIM), router.T,
        first_weight[0], second_weight[0],
    )
    token_grad, router_column, first_grad, second_grad = pl.pallas_call(
        store_kernel,
        out_shape=(
            jax.ShapeDtypeStruct((IMG * TOK, DIM), BF16),
            jax.ShapeDtypeStruct((1, DIM), F32),
            jax.ShapeDtypeStruct((DIM, HID), BF16),
            jax.ShapeDtypeStruct((HID, DIM), BF16),
        ),
        in_specs=[pl.BlockSpec(memory_space=pltpu.VMEM)] * 4,
        out_specs=(
            pl.BlockSpec(memory_space=pl.ANY),
            pl.BlockSpec(memory_space=pltpu.VMEM),
            pl.BlockSpec(memory_space=pl.ANY),
            pl.BlockSpec(memory_space=pl.ANY),
        ),
        scratch_shapes=[dma((3,))],
        compiler_params=pltpu.CompilerParams(vmem_limit_bytes=8 * 1024 * 1024),
    )(*results)
    return (
        token_grad.reshape(IMG, TOK, DIM),
        router_column.reshape(DIM, 1),
        first_grad[None],
        second_grad[None],
    )


def solution(mesh):
    placed = (
        P(("dp", "expert"), None, None),
        P(("dp", "expert"), None, None),
        P(),
        P("expert", None, "dp"),
        P("expert", "dp", None),
    )
    return jax.shard_map(
        body,
        mesh=mesh,
        in_specs=placed,
        out_specs=(
            P(("dp", "expert"), None, None),
            P(None, "expert"),
            P("expert", None, "dp"),
            P("expert", "dp", None),
        ),
        check_vma=False,
    )
```

```python
import functools

import jax
import jax.numpy as jnp
from jax import lax
from jax.experimental import pallas as pl
from jax.experimental.pallas import tpu as pltpu
from jax.sharding import PartitionSpec as P

ROOT_TWO_OVER_PI = 0.7978845608028654
CUBIC_TERM = 0.044715
MESH = pl.DeviceIdType.MESH
F32, BF16 = jnp.float32, jnp.bfloat16

NZ, NYX = 8, 8
IMG, TOK, DIM, HID, EXP = 2, 256, 1280, 640, 64
CW = 256
NC = DIM // CW
N_BLK = 4
UNITS = 2 * NC
LAST = 38


def mm(a, b):
    return lax.dot_general(a, b, (((1,), (0,)), ((), ())), preferred_element_type=F32)


def mm_nt(a, b):
    return lax.dot_general(a, b, (((1,), (1,)), ((), ())), preferred_element_type=F32)


def mm_tn(a, b):
    return lax.dot_general(a, b, (((0,), (0,)), ((), ())), preferred_element_type=F32)


def iota(shape, axis):
    return lax.broadcasted_iota(jnp.int32, shape, axis)


def one_hot(mask):
    return jnp.where(mask, 1.0, 0.0).astype(BF16)


def kernel(
    tok_hbm, cot_hbm, rt_hbm, w1_hbm, w2_hbm,
    tgv, rg_out, g1v, g2v,
    tok, cot, rt, rtj, w1, w2, ltm, disp, comb, dlow, perm1, perm3,
    send1, recv1, send2, xs, acc_pre, acc_act, hid, pg,
    op, rc, t_own, sx, rx, so, ry, sz, rz, rp, cgx, dgx, low2,
    rsend, rrecv, rs2, rr2, rs3, rr3,
    in_sem, z1_sem, y1_sem, agx_sem, agc_sem, agd_sem,
    rc_sem, rx_sem, ry_sem, rz_sem, rt_sem, snd_sem,
):
    p = lax.axis_index("dp")
    q = lax.axis_index("expert")
    z = lax.rem(q, NZ)
    yx = lax.div(q, NZ)
    y = lax.div(yx, 2)
    xh = lax.rem(yx, 2)

    z_at = [lax.rem(z + far, NZ) for far in (1, 7, 2, 6, 3, 5, 4)]
    z_peers = [(zt, (p, yx * NZ + zt)) for zt in z_at]
    p_flip = lax.rem(p + 2, 4)
    p_at, xh_at = (p, p_flip), (xh, 1 - xh)

    def yx_peer(dy, dx):
        yxt = lax.rem(y + dy, 4) * 2 + xh_at[dx]
        return yxt, (p_at[dx], yxt * NZ + z)

    yx_peers = [yx_peer(k // 2, k % 2) for k in range(1, 8)]
    core_peer = (p + 1 - 2 * lax.rem(p, 2), q)
    x_peer = (p_flip, q)
    dp_peers = [(lax.rem(p + k, 4), q) for k in range(1, 4)]

    def remote(src, dst, send_sem, recv_sem, dev):
        pltpu.make_async_remote_copy(
            src_ref=src, dst_ref=dst, send_sem=send_sem, recv_sem=recv_sem,
            device_id=dev, device_id_type=MESH,
        ).start()

    def await_bytes(ref, sem):
        pltpu.make_async_copy(ref, ref, sem).wait()

    def split(u):
        c = lax.rem(u, NC)
        return lax.div(u, NC), c, pl.ds(pl.multiple_of(c * CW, CW), CW)

    def rows_at(index, size):
        return pl.ds(pl.multiple_of(index * size, size), size)

    loads = [
        pltpu.make_async_copy(a, b, in_sem.at[i])
        for i, (a, b) in enumerate(
            ((rt_hbm, rt), (tok_hbm, tok), (cot_hbm, cot), (w1_hbm, w1), (w2_hbm, w2))
        )
    ]
    for load in loads[:3]:
        load.start()

    barrier = pltpu.get_barrier_semaphore()

    for dev in [dev for _, dev in z_peers + yx_peers] + dp_peers:
        pl.semaphore_signal(barrier, inc=1, device_id=dev, device_id_type=MESH)

    o1, n1 = iota((128, 128), 0), iota((128, 128), 1)
    perm1[...] = one_hot(
        n1 == ((o1 >> 1) & 7) * 16 + ((o1 >> 4) & 3) * 4 + (o1 >> 6) * 2 + (o1 & 1)
    )
    perm3[...] = one_hot(n1 == (o1 & 31) * 4 + ((o1 >> 5) & 1) * 2 + (o1 >> 6))

    def expert_of(j):
        y_at = (y + (j >> 5) * 2 + ((j >> 1) & 1)) & 3
        return (y_at * 2 + ((xh + j) & 1)) * 8 + ((j >> 2) & 7)

    n2, j2 = iota((256, EXP), 0), iota((256, EXP), 1)
    same_slot = j2 == n2 >> 2

    loads[0].wait()
    by_slot = one_hot(iota((EXP, EXP), 1) == expert_of(iota((EXP, EXP), 0)))
    rtj[...] = mm(by_slot, rt[...]).astype(BF16)
    loads[1].wait()
    loads[3].start()
    loads[4].start()
    logits = mm_nt(tok[...], rtj[...])
    for i in range(IMG):
        rows = pl.ds(i * TOK, TOK)
        part = logits[i * TOK:(i + 1) * TOK]
        up = jnp.exp(part - jnp.max(part, axis=0, keepdims=True))
        d = up / jnp.sum(up, axis=0, keepdims=True)
        up = jnp.exp(part - jnp.max(part, axis=1, keepdims=True))
        c = up / jnp.sum(up, axis=1, keepdims=True)
        disp[rows, :] = d
        comb[rows, :] = c
        d_low = d.astype(BF16)
        dlow[rows, :] = d_low
        for a, low in ((0, d_low), (1, c.astype(BF16))):
            spread = one_hot(same_slot & ((n2 & 3) == a * 2 + i))
            ltm[:, pl.ds(a * 512 + i * TOK, TOK)] = mm_nt(spread, low).astype(BF16)
    loads[2].wait()
    pl.semaphore_wait(barrier, 17)

    def send_slots(u):
        h, c, ch = split(u)
        rows = rows_at(h, 128)
        send1[u] = (
            mm(ltm[rows, :512], tok[:, ch]) + mm(ltm[rows, 512:], cot[:, ch])
        ).astype(BF16)
        mine = rows_at(z, 16)
        recv1[u, mine] = send1[u, mine]

        for zt, dev in z_peers:
            remote(
                send1.at[u, rows_at(zt, 16)], recv1.at[u, mine],
                snd_sem.at[0], z1_sem.at[u], dev,
            )

    def to_neighbours(h, src, dst, send_sem, recv_sem, sign):
        @pl.when(h == 0)
        def _():
            pltpu.make_async_copy(src(0), dst(0), recv_sem).start()

        @pl.when(h == 1)
        def _():
            remote(src(0), dst(0), send_sem, recv_sem, yx_peer(2, 0)[1])

        start = 2 * h if sign > 0 else 8 - 2 * h
        for k in range(1, 4):
            remote(src(k), dst(k), send_sem, recv_sem, yx_peer(start + sign * (k // 2), k % 2)[1])

    def turn_slots(u):
        h, c, ch = split(u)
        await_bytes(recv1.at[u, pl.ds(0, 112)], z1_sem.at[u])
        send2[u] = mm(perm1[...], recv1[u]).astype(BF16).reshape(2, 64, CW)
        to_neighbours(
            h, lambda k: send2.at[u, :, rows_at(k, 16)],
            lambda k: xs.at[u, 0, :, rows_at(k, 16)], snd_sem.at[1], y1_sem.at[u], 1,
        )

    def gather_slots(u):
        h, c, ch = split(u)
        await_bytes(xs.at[u, 0], y1_sem.at[u])
        remote(xs.at[u, 0], xs.at[u, 1], snd_sem.at[2], agx_sem.at[u], x_peer)
        remote(xs.at[u, 0], xs.at[u, 2], snd_sem.at[3], agc_sem.at[u], core_peer)

    def forward_slots(u):
        h, c, ch = split(u)
        await_bytes(xs.at[u, 1], agx_sem.at[u])
        remote(xs.at[u, 1], xs.at[u, 3], snd_sem.at[4], agd_sem.at[u], core_peer)

    def first_layer(u):
        h, c, ch = split(u)
        await_bytes(xs.at[u, 2], agc_sem.at[u])
        await_bytes(xs.at[u, 3], agd_sem.at[u])
        acc_pre[h] += mm(xs[u, :, 0].reshape(256, CW), w1[ch, :])
        acc_act[h] += mm_nt(xs[u, :, 1].reshape(256, CW), w2[:, ch])

        @pl.when(c == NC - 1)
        def _():
            @pl.loop(0, 4)
            def _(b):
                rows = rows_at(b, 64)
                v = acc_pre[h, rows, :]
                square = v * v
                tangent = jnp.tanh(ROOT_TWO_OVER_PI * (v + CUBIC_TERM * square * v))
                hid[h, rows, :] = (0.5 * v * (1.0 + tangent)).astype(BF16)
                slope = 0.5 * (1.0 + tangent) + 0.5 * v * (
                    1.0 - tangent * tangent
                ) * ROOT_TWO_OVER_PI * (1.0 + 3.0 * CUBIC_TERM * square)
                pg[h, rows, :] = (acc_act[h, rows, :] * slope).astype(BF16)

    def second_layer(u):
        h, c, ch = split(u)
        op[u, :, 0] = mm(hid[h], w2[:, ch]).astype(BF16).reshape(N_BLK, 64, CW)
        op[u, :, 1] = mm_nt(pg[h], w1[ch, :]).astype(BF16).reshape(N_BLK, 64, CW)
        remote(
            op.at[u, pl.ds(2, 2)], rc.at[u],
            snd_sem.at[5], rc_sem.at[u], core_peer,
        )

    def core_sum(u):
        h, c, ch = split(u)
        await_bytes(rc.at[u], rc_sem.at[u])
        sx[u] = (
            op[u, 1].astype(F32) + rc[u, 1].astype(F32)
        ).astype(BF16)
        remote(sx.at[u], rx.at[u], snd_sem.at[6], rx_sem.at[u], x_peer)
        t_own[u] = op[u, 0].astype(F32) + rc[u, 0].astype(F32)

    def weight_grads(c):
        ch = pl.ds(pl.multiple_of(c * CW, CW), CW)
        g1v[ch, :] = (
            mm_tn(xs[c, :, 0].reshape(256, CW), pg[0])
            + mm_tn(xs[NC + c, :, 0].reshape(256, CW), pg[1])
        ).astype(BF16)
        g2v[:, ch] = (
            mm_tn(hid[0], xs[c, :, 1].reshape(256, CW))
            + mm_tn(hid[1], xs[NC + c, :, 1].reshape(256, CW))
        ).astype(BF16)

    def x_sum(u):
        h, c, ch = split(u)
        await_bytes(rx.at[u], rx_sem.at[u])
        so[u] = (t_own[u] + rx[u].astype(F32)).astype(BF16)
        to_neighbours(
            h, lambda k: so.at[u, :, rows_at(k, 16)],
            lambda k: ry.at[u, :, rows_at(k, 16)], snd_sem.at[7], ry_sem.at[u], -1,
        )

    def turn_back(u):
        h, c, ch = split(u)
        await_bytes(ry.at[u], ry_sem.at[u])
        sz[u] = mm_tn(perm1[...], ry[u].reshape(128, CW)).astype(BF16)
        mine = rows_at(z, 16)
        rz[u, mine] = sz[u, mine]

        for zt, dev in z_peers:
            remote(
                sz.at[u, rows_at(zt, 16)], rz.at[u, mine],
                snd_sem.at[8], rz_sem.at[u], dev,
            )

    def slots_back(u):
        h, c, ch = split(u)
        await_bytes(rz.at[u, pl.ds(0, 112)], rz_sem.at[u])
        rp[h, :, ch] = mm(perm3[...], rz[u]).astype(BF16)
        for i in range(IMG):
            rows = pl.ds(i * TOK, TOK)
            slots = rp[h, pl.ds(i * 64, 64), ch]
            cgx[h, rows, :] += mm_nt(cot[rows, ch], slots)
            dgx[h, rows, :] += mm_nt(tok[rows, ch], slots)

    @pl.loop(0, LAST)
    def _(step):
        for lag, count, stage in (
            (0, UNITS, send_slots), (16, UNITS, second_layer), (23, UNITS, turn_back),
            (7, UNITS, gather_slots), (20, UNITS, x_sum), (31, NC, weight_grads),
            (4, UNITS, turn_slots), (28, UNITS, slots_back), (10, UNITS, forward_slots),
            (17, UNITS, core_sum), (11, UNITS, first_layer),
        ):
            @pl.when((step >= lag) & (step < lag + count))
            def _(stage=stage, lag=lag):
                stage(step - lag)

        @pl.when(step == 0)
        def _():
            for ref in (acc_pre, acc_act, cgx, dgx):
                ref[...] = jnp.zeros_like(ref)
            loads[3].wait()
            loads[4].wait()

    c_grads = jnp.concatenate([cgx[0, :, :32], cgx[1, :, :32]], axis=1)
    d_grads = jnp.concatenate([dgx[0, :, 32:], dgx[1, :, 32:]], axis=1)
    for i in range(IMG):
        rows = pl.ds(i * TOK, TOK)
        d, c = disp[rows, :], comb[rows, :]
        d_grad, c_grad = d_grads[i * TOK:(i + 1) * TOK], c_grads[i * TOK:(i + 1) * TOK]
        grad = d * (d_grad - jnp.sum(d * d_grad, axis=0, keepdims=True))
        grad = grad + c * (c_grad - jnp.sum(c * c_grad, axis=1, keepdims=True))
        low2[rows, :64] = dlow[rows, :]
        low2[rows, 64:] = grad.astype(BF16)

    e3, j3 = iota((EXP, EXP), 1), iota((EXP, EXP), 0)
    by_z = one_hot(expert_of(j3) == (e3 & 7) * 8 + (e3 >> 3))
    turned = mm(low2[:, 64:], by_z).astype(BF16)
    part = mm_tn(turned, tok[...])
    for k in range(NZ):
        rows = part[k * 8:(k + 1) * 8]
        rsend[pl.ds(k * 16, 16), :] = jnp.concatenate(
            [rows[:, :HID], rows[:, HID:]], axis=0
        ).astype(BF16)
    mine_z = rows_at(z, 16)
    pltpu.make_async_copy(rsend.at[mine_z], rrecv.at[mine_z], rt_sem.at[0]).start()

    for zt, dev in z_peers:
        remote(rsend.at[rows_at(zt, 16)], rrecv.at[mine_z], snd_sem.at[9], rt_sem.at[0], dev)

    for i in range(IMG):
        rows = pl.ds(i * TOK, TOK)

        @pl.loop(0, NC)
        def _(c, i=i, rows=rows):
            ch = pl.ds(pl.multiple_of(c * CW, CW), CW)
            back = pl.ds(i * 64 + 32, 32)
            right = jnp.concatenate([rp[0, back, ch], rp[1, back, ch], rtj[:, ch]], axis=0)
            tgv[rows, ch] = mm(low2[rows, :], right).astype(BF16)

    await_bytes(rrecv, rt_sem.at[0])
    total = rrecv[pl.ds(0, 16), :].astype(F32)
    for k in range(1, NZ):
        total = total + rrecv[pl.ds(k * 16, 16), :].astype(F32)
    for k in range(NYX):
        rs2[k, pl.ds(0, 1), :] = total[k:k + 1]
        rs2[k, pl.ds(1, 1), :] = total[8 + k:9 + k]
    pltpu.make_async_copy(rs2.at[yx], rr2.at[yx], rt_sem.at[1]).start()

    for yxt, dev in yx_peers:
        remote(rs2.at[yxt], rr2.at[yx], snd_sem.at[10], rt_sem.at[1], dev)

    await_bytes(rr2, rt_sem.at[1])
    rs3[...] = jnp.sum(rr2[...], axis=0)
    pltpu.make_async_copy(rs3, rr3.at[p], rt_sem.at[2]).start()
    for dev in dp_peers:
        remote(rs3, rr3.at[p], snd_sem.at[11], rt_sem.at[2], dev)
    await_bytes(rr3, rt_sem.at[2])
    rg_out[...] = (rr3[0] + rr3[1]) + (rr3[2] + rr3[3])

    seven = send1.at[:, pl.ds(0, 112)]
    for ref, number in (
        (seven, 0), (seven, 1), (xs.at[:, 0], 2), (xs.at[:, 0], 3), (xs.at[:, 1], 4),
        (rc, 5), (sx, 6), (seven, 7), (seven, 8),
        (rsend.at[pl.ds(0, 112)], 9), (rs2.at[pl.ds(0, 7)], 10), (rr3.at[pl.ds(0, 3)], 11),
    ):
        await_bytes(ref, snd_sem.at[number])


def store_kernel(tg, rg, g1, g2, tg_hbm, rg_out, g1_hbm, g2_hbm, sem):
    stores = [
        pltpu.make_async_copy(a, b, sem.at[i])
        for i, (a, b) in enumerate(((g1, g1_hbm), (g2, g2_hbm), (tg, tg_hbm)))
    ]
    for store in stores:
        store.start()
    rg_out[:, :HID] = rg[0:1, :]
    rg_out[:, HID:] = rg[1:2, :]
    for store in stores:
        store.wait()


def body(tokens, cotangent, router, first_weight, second_weight):
    vmem, dma = pltpu.VMEM, pltpu.SemaphoreType.DMA
    results = pl.pallas_call(
        kernel,
        out_shape=(
            vmem((IMG * TOK, DIM), BF16),
            vmem((2, HID), F32),
            vmem((DIM, HID), BF16),
            vmem((HID, DIM), BF16),
        ),
        in_specs=[pl.BlockSpec(memory_space=pltpu.HBM)] * 5,
        out_specs=(pl.BlockSpec(memory_space=pltpu.VMEM),) * 4,
        scratch_shapes=[
            vmem((IMG * TOK, DIM), BF16),
            vmem((IMG * TOK, DIM), BF16),
            vmem((EXP, DIM), BF16),
            vmem((EXP, DIM), BF16),
            vmem((DIM, HID), BF16),
            vmem((HID, DIM), BF16),
            vmem((256, 1024), BF16),
            vmem((IMG * TOK, EXP), F32),
            vmem((IMG * TOK, EXP), F32),
            vmem((IMG * TOK, EXP), BF16),
            vmem((128, 128), BF16),
            vmem((128, 128), BF16),
            vmem((UNITS, 128, CW), BF16),
            vmem((UNITS, 128, CW), BF16),
            vmem((UNITS, 2, 64, CW), BF16),
            vmem((UNITS, N_BLK, 2, 64, CW), BF16),
            vmem((2, 256, HID), F32),
            vmem((2, 256, HID), F32),
            vmem((2, 256, HID), BF16),
            vmem((2, 256, HID), BF16),
            vmem((UNITS, N_BLK, 2, 64, CW), BF16),
            vmem((UNITS, 2, 2, 64, CW), BF16),
            vmem((UNITS, 2, 64, CW), F32),
            vmem((UNITS, 2, 64, CW), BF16),
            vmem((UNITS, 2, 64, CW), BF16),
            vmem((UNITS, 2, 64, CW), BF16),
            vmem((UNITS, 2, 64, CW), BF16),
            vmem((UNITS, 128, CW), BF16),
            vmem((UNITS, 128, CW), BF16),
            vmem((2, 128, DIM), BF16),
            vmem((2, IMG * TOK, EXP), F32),
            vmem((2, IMG * TOK, EXP), F32),
            vmem((IMG * TOK, 2 * EXP), BF16),
            vmem((NZ * 16, HID), BF16),
            vmem((NZ * 16, HID), BF16),
            vmem((NYX, 2, HID), F32),
            vmem((NYX, 2, HID), F32),
            vmem((2, HID), F32),
            vmem((4, 2, HID), F32),
            dma((5,)),
            dma((UNITS,)), dma((UNITS,)), dma((UNITS,)), dma((UNITS,)), dma((UNITS,)),
            dma((UNITS,)), dma((UNITS,)), dma((UNITS,)), dma((UNITS,)),
            dma((3,)), dma((12,)),
        ],
        compiler_params=pltpu.CompilerParams(
            collective_id=0, has_side_effects=True, vmem_limit_bytes=56 * 1024 * 1024
        ),
    )(
        tokens.reshape(IMG * TOK, DIM), cotangent.reshape(IMG * TOK, DIM), router.T,
        first_weight[0], second_weight[0],
    )
    token_grad, router_column, first_grad, second_grad = pl.pallas_call(
        store_kernel,
        out_shape=(
            jax.ShapeDtypeStruct((IMG * TOK, DIM), BF16),
            jax.ShapeDtypeStruct((1, DIM), F32),
            jax.ShapeDtypeStruct((DIM, HID), BF16),
            jax.ShapeDtypeStruct((HID, DIM), BF16),
        ),
        in_specs=[pl.BlockSpec(memory_space=pltpu.VMEM)] * 4,
        out_specs=(
            pl.BlockSpec(memory_space=pl.ANY),
            pl.BlockSpec(memory_space=pltpu.VMEM),
            pl.BlockSpec(memory_space=pl.ANY),
            pl.BlockSpec(memory_space=pl.ANY),
        ),
        scratch_shapes=[dma((3,))],
        compiler_params=pltpu.CompilerParams(vmem_limit_bytes=8 * 1024 * 1024),
    )(*results)
    return (
        token_grad.reshape(IMG, TOK, DIM),
        router_column.reshape(DIM, 1),
        first_grad[None],
        second_grad[None],
    )


def solution(mesh):
    placed = (
        P(("dp", "expert"), None, None),
        P(("dp", "expert"), None, None),
        P(),
        P("expert", None, "dp"),
        P("expert", "dp", None),
    )
    return jax.shard_map(
        body,
        mesh=mesh,
        in_specs=placed,
        out_specs=(
            P(("dp", "expert"), None, None),
            P(None, "expert"),
            P("expert", None, "dp"),
            P("expert", "dp", None),
        ),
        check_vma=False,
    )
```

```python
import functools

import jax
import jax.numpy as jnp
from jax import lax
from jax.experimental import pallas as pl
from jax.experimental.pallas import tpu as pltpu
from jax.sharding import PartitionSpec as P

ROOT_TWO_OVER_PI = 0.7978845608028654
CUBIC_TERM = 0.044715
MESH = pl.DeviceIdType.MESH
F32, BF16 = jnp.float32, jnp.bfloat16

NZ, NYX = 8, 8
IMG, TOK, DIM, HID, EXP = 2, 256, 1280, 640, 64
CW = 256
NC = DIM // CW
N_BLK = 4
UNITS = 2 * NC
LAST = 38


def mm(a, b):
    return lax.dot_general(a, b, (((1,), (0,)), ((), ())), preferred_element_type=F32)


def mm_nt(a, b):
    return lax.dot_general(a, b, (((1,), (1,)), ((), ())), preferred_element_type=F32)


def mm_tn(a, b):
    return lax.dot_general(a, b, (((0,), (0,)), ((), ())), preferred_element_type=F32)


def iota(shape, axis):
    return lax.broadcasted_iota(jnp.int32, shape, axis)


def one_hot(mask):
    return jnp.where(mask, 1.0, 0.0).astype(BF16)


def kernel(
    tok_hbm, cot_hbm, rt_hbm, w1_hbm, w2_hbm,
    tgv, rg_out, g1v, g2v,
    tok, cot, rt, rtj, w1, w2, ltm, disp, comb, dlow, perm1, perm3,
    send1, recv1, send2, xs, acc_pre, acc_act, hid, pg,
    op, rc, t_own, sx, rx, so, ry, sz, rz, rp, cgx, dgx, low2,
    rsend, rrecv, rs2, rr2, rr3,
    in_sem, z1_sem, y1_sem, agx_sem, agc_sem,
    rc_sem, rx_sem, ry_sem, rz_sem, rt_sem, snd_sem,
):
    p = lax.axis_index("dp")
    q = lax.axis_index("expert")
    z = lax.rem(q, NZ)
    yx = lax.div(q, NZ)
    y = lax.div(yx, 2)
    xh = lax.rem(yx, 2)

    z_at = [lax.rem(z + far, NZ) for far in (4, 3, 5, 2, 6, 1, 7)]
    z_peers = [(zt, (p, yx * NZ + zt)) for zt in z_at]
    p_flip = lax.rem(p + 2, 4)
    p_at, xh_at = (p, p_flip), (xh, 1 - xh)

    def yx_peer(dy, dx):
        yxt = lax.rem(y + dy, 4) * 2 + xh_at[dx]
        return yxt, (p_at[dx], yxt * NZ + z)

    yx_peers = [yx_peer(k // 2, k % 2) for k in range(1, 8)]
    core_peer = (p + 1 - 2 * lax.rem(p, 2), q)
    x_peer = (p_flip, q)
    dp_peers = [(lax.rem(p + k, 4), q) for k in range(1, 4)]

    def remote(src, dst, send_sem, recv_sem, dev):
        pltpu.make_async_remote_copy(
            src_ref=src, dst_ref=dst, send_sem=send_sem, recv_sem=recv_sem,
            device_id=dev, device_id_type=MESH,
        ).start()

    def await_bytes(ref, sem):
        pltpu.make_async_copy(ref, ref, sem).wait()

    def split(u):
        c = lax.rem(u, NC)
        return lax.div(u, NC), c, pl.ds(pl.multiple_of(c * CW, CW), CW)

    def rows_at(index, size):
        return pl.ds(pl.multiple_of(index * size, size), size)

    loads = [
        pltpu.make_async_copy(a, b, in_sem.at[i])
        for i, (a, b) in enumerate(
            ((rt_hbm, rt), (tok_hbm, tok), (cot_hbm, cot), (w1_hbm, w1), (w2_hbm, w2))
        )
    ]
    for load in loads[:3]:
        load.start()

    barrier = pltpu.get_barrier_semaphore()

    column = [(pt, yx * NZ + zt) for zt in z_at for pt, _ in dp_peers]
    for dev in [dev for _, dev in z_peers + yx_peers] + dp_peers + column:
        pl.semaphore_signal(barrier, inc=1, device_id=dev, device_id_type=MESH)

    o1, n1 = iota((128, 128), 0), iota((128, 128), 1)
    perm1[...] = one_hot(
        n1 == ((o1 >> 1) & 7) * 16 + ((o1 >> 4) & 3) * 4 + (o1 >> 6) * 2 + (o1 & 1)
    )
    perm3[...] = one_hot(n1 == (o1 & 31) * 4 + ((o1 >> 5) & 1) * 2 + (o1 >> 6))

    def expert_of(j):
        y_at = (y + (j >> 5) * 2 + ((j >> 1) & 1)) & 3
        return (y_at * 2 + ((xh + j) & 1)) * 8 + ((j >> 2) & 7)

    n2, j2 = iota((256, EXP), 0), iota((256, EXP), 1)
    same_slot = j2 == n2 >> 2

    loads[0].wait()
    by_slot = one_hot(iota((EXP, EXP), 1) == expert_of(iota((EXP, EXP), 0)))
    rtj[...] = mm(by_slot, rt[...]).astype(BF16)
    loads[1].wait()
    loads[3].start()
    loads[4].start()
    logits = mm_nt(tok[...], rtj[...])
    for i in range(IMG):
        rows = pl.ds(i * TOK, TOK)
        part = logits[i * TOK:(i + 1) * TOK]
        up = jnp.exp(part - jnp.max(part, axis=0, keepdims=True))
        d = up / jnp.sum(up, axis=0, keepdims=True)
        up = jnp.exp(part - jnp.max(part, axis=1, keepdims=True))
        c = up / jnp.sum(up, axis=1, keepdims=True)
        disp[rows, :] = d
        comb[rows, :] = c
        d_low = d.astype(BF16)
        dlow[rows, :] = d_low
        for a, low in ((0, d_low), (1, c.astype(BF16))):
            spread = one_hot(same_slot & ((n2 & 3) == a * 2 + i))
            ltm[:, pl.ds(a * 512 + i * TOK, TOK)] = mm_nt(spread, low).astype(BF16)
    loads[2].wait()
    pl.semaphore_wait(barrier, 38)

    def send_slots(u):
        h, c, ch = split(u)
        rows = rows_at(h, 128)
        send1[u] = (
            mm(ltm[rows, :512], tok[:, ch]) + mm(ltm[rows, 512:], cot[:, ch])
        ).astype(BF16)
        mine = rows_at(z, 16)
        recv1[u, mine] = send1[u, mine]

        for zt, dev in z_peers:
            remote(
                send1.at[u, rows_at(zt, 16)], recv1.at[u, mine],
                snd_sem.at[0], z1_sem.at[u], dev,
            )

    def to_neighbours(h, src, dst, send_sem, recv_sem, sign):
        @pl.when(h == 1)
        def _():
            remote(src(0), dst(0), send_sem, recv_sem, yx_peer(2, 0)[1])

        start = 2 * h if sign > 0 else 8 - 2 * h
        for k in range(1, 4):
            remote(src(k), dst(k), send_sem, recv_sem, yx_peer(start + sign * (k // 2), k % 2)[1])

    def await_neighbours(h, ref, sem):
        @pl.when(h == 0)
        def _():
            await_bytes(ref.at[:, pl.ds(0, 48)], sem)

        @pl.when(h == 1)
        def _():
            await_bytes(ref, sem)

    def turn_slots(u):
        h, c, ch = split(u)
        await_bytes(recv1.at[u, pl.ds(0, 112)], z1_sem.at[u])
        send2[u] = mm(perm1[...], recv1[u]).astype(BF16).reshape(2, 64, CW)

        @pl.when(h == 0)
        def _():
            xs[u, 0, :, :16] = send2[u, :, :16]

        to_neighbours(
            h, lambda k: send2.at[u, :, rows_at(k, 16)],
            lambda k: xs.at[u, 0, :, rows_at(k, 16)], snd_sem.at[1], y1_sem.at[u], 1,
        )

    def gather_slots(u):
        h, c, ch = split(u)
        await_neighbours(h, xs.at[u, 0], y1_sem.at[u])
        remote(xs.at[u, 0], xs.at[u, 1], snd_sem.at[2], agx_sem.at[u], x_peer)

    def forward_slots(u):
        h, c, ch = split(u)
        await_bytes(xs.at[u, 1], agx_sem.at[u])
        remote(
            xs.at[u, pl.ds(0, 2)], xs.at[u, pl.ds(2, 2)], snd_sem.at[3], agc_sem.at[u], core_peer
        )

    def first_layer(u):
        h, c, ch = split(u)
        await_bytes(xs.at[u, pl.ds(2, 2)], agc_sem.at[u])
        acc_pre[h] += mm(xs[u, :, 0].reshape(256, CW), w1[ch, :])
        acc_act[h] += mm_nt(xs[u, :, 1].reshape(256, CW), w2[:, ch])

        @pl.when(c == NC - 1)
        def _():
            @pl.loop(0, 4)
            def _(b):
                rows = rows_at(b, 64)
                v = acc_pre[h, rows, :]
                square = v * v
                tangent = jnp.tanh(ROOT_TWO_OVER_PI * (v + CUBIC_TERM * square * v))
                hid[h, rows, :] = (0.5 * v * (1.0 + tangent)).astype(BF16)
                slope = 0.5 * (1.0 + tangent) + 0.5 * v * (
                    1.0 - tangent * tangent
                ) * ROOT_TWO_OVER_PI * (1.0 + 3.0 * CUBIC_TERM * square)
                pg[h, rows, :] = (acc_act[h, rows, :] * slope).astype(BF16)

    def second_layer(u):
        h, c, ch = split(u)
        op[u, :, 0] = mm(hid[h], w2[:, ch]).astype(BF16).reshape(N_BLK, 64, CW)
        op[u, :, 1] = mm_nt(pg[h], w1[ch, :]).astype(BF16).reshape(N_BLK, 64, CW)
        remote(
            op.at[u, pl.ds(2, 2)], rc.at[u],
            snd_sem.at[5], rc_sem.at[u], core_peer,
        )

    def core_sum(u):
        h, c, ch = split(u)
        await_bytes(rc.at[u], rc_sem.at[u])
        sx[u] = (
            op[u, 1].astype(F32) + rc[u, 1].astype(F32)
        ).astype(BF16)
        remote(sx.at[u], rx.at[u], snd_sem.at[6], rx_sem.at[u], x_peer)
        t_own[u] = op[u, 0].astype(F32) + rc[u, 0].astype(F32)

    def weight_grads(c):
        ch = pl.ds(pl.multiple_of(c * CW, CW), CW)
        g1v[ch, :] = (
            mm_tn(xs[c, :, 0].reshape(256, CW), pg[0])
            + mm_tn(xs[NC + c, :, 0].reshape(256, CW), pg[1])
        ).astype(BF16)
        g2v[:, ch] = (
            mm_tn(hid[0], xs[c, :, 1].reshape(256, CW))
            + mm_tn(hid[1], xs[NC + c, :, 1].reshape(256, CW))
        ).astype(BF16)

    def x_sum(u):
        h, c, ch = split(u)
        await_bytes(rx.at[u], rx_sem.at[u])
        so[u] = (t_own[u] + rx[u].astype(F32)).astype(BF16)

        @pl.when(h == 0)
        def _():
            ry[u, :, :16] = so[u, :, :16]

        to_neighbours(
            h, lambda k: so.at[u, :, rows_at(k, 16)],
            lambda k: ry.at[u, :, rows_at(k, 16)], snd_sem.at[7], ry_sem.at[u], -1,
        )

    def turn_back(u):
        h, c, ch = split(u)
        await_neighbours(h, ry.at[u], ry_sem.at[u])
        sz[u] = mm_tn(perm1[...], ry[u].reshape(128, CW)).astype(BF16)
        mine = rows_at(z, 16)
        rz[u, mine] = sz[u, mine]

        for zt, dev in z_peers:
            remote(
                sz.at[u, rows_at(zt, 16)], rz.at[u, mine],
                snd_sem.at[8], rz_sem.at[u], dev,
            )

    def slots_back(u):
        h, c, ch = split(u)
        await_bytes(rz.at[u, pl.ds(0, 112)], rz_sem.at[u])
        rp[h, :, ch] = mm(perm3[...], rz[u]).astype(BF16)
        for i in range(IMG):
            rows = pl.ds(i * TOK, TOK)
            slots = rp[h, pl.ds(i * 64, 64), ch]
            cgx[h, rows, :] += mm_nt(cot[rows, ch], slots)
            dgx[h, rows, :] += mm_nt(tok[rows, ch], slots)

    @pl.loop(0, LAST)
    def _(step):
        for lag, count, stage in (
            (0, UNITS, send_slots), (16, UNITS, second_layer), (23, UNITS, turn_back),
            (7, UNITS, gather_slots), (20, UNITS, x_sum), (4, UNITS, turn_slots),
            (28, UNITS, slots_back), (31, NC, weight_grads), (10, UNITS, forward_slots),
            (17, UNITS, core_sum), (11, UNITS, first_layer),
        ):
            @pl.when((step >= lag) & (step < lag + count))
            def _(stage=stage, lag=lag):
                stage(step - lag)

        @pl.when(step == 0)
        def _():
            for ref in (acc_pre, acc_act, cgx, dgx):
                ref[...] = jnp.zeros_like(ref)
            loads[3].wait()
            loads[4].wait()

    c_grads = jnp.concatenate([cgx[0, :, :32], cgx[1, :, :32]], axis=1)
    d_grads = jnp.concatenate([dgx[0, :, 32:], dgx[1, :, 32:]], axis=1)
    for i in range(IMG):
        rows = pl.ds(i * TOK, TOK)
        d, c = disp[rows, :], comb[rows, :]
        d_grad, c_grad = d_grads[i * TOK:(i + 1) * TOK], c_grads[i * TOK:(i + 1) * TOK]
        grad = d * (d_grad - jnp.sum(d * d_grad, axis=0, keepdims=True))
        grad = grad + c * (c_grad - jnp.sum(c * c_grad, axis=1, keepdims=True))
        low2[rows, :64] = dlow[rows, :]
        low2[rows, 64:] = grad.astype(BF16)

    all_but_one = rr3.at[pl.ds(0, 31)]

    r3, j3 = iota((EXP, EXP), 1), iota((EXP, EXP), 0)
    by_peer = one_hot(j3 == (r3 >> 5) * 32 + (r3 & 7) * 4 + ((r3 >> 3) & 3))
    turned = mm(low2[:, 64:], by_peer).astype(BF16)
    part = mm_tn(turned, tok[...])
    for k in range(NYX):
        rows = part[k * 8:(k + 1) * 8]
        rsend[pl.ds(k * 16, 16), :] = jnp.concatenate(
            [rows[:, :HID], rows[:, HID:]], axis=0
        ).astype(BF16)
    for k, (_, dev) in enumerate(yx_peers, 1):
        rows = pl.ds(k * 16, 16)
        remote(rsend.at[rows], rrecv.at[rows], snd_sem.at[9], rt_sem.at[0], dev)

    await_bytes(rrecv.at[pl.ds(16, 112)], rt_sem.at[0])
    total = rsend[pl.ds(0, 16), :].astype(F32)
    for k in range(1, NYX):
        total = total + rrecv[pl.ds(k * 16, 16), :].astype(F32)
    for k in range(NZ):
        rs2[k, pl.ds(0, 1), :] = total[k:k + 1]
        rs2[k, pl.ds(1, 1), :] = total[8 + k:9 + k]
    for zt in [z] + z_at:
        for pt in [p] + [pt for pt, _ in dp_peers]:
            if zt is not z or pt is not p:
                remote(
                    rs2.at[zt], rr2.at[p, z], snd_sem.at[10], rt_sem.at[1], (pt, yx * NZ + zt)
                )
    rr2[p, z] = rs2[z]

    for i in range(IMG):
        rows = pl.ds(i * TOK, TOK)

        @pl.loop(0, NC)
        def _(c, i=i, rows=rows):
            ch = pl.ds(pl.multiple_of(c * CW, CW), CW)
            back = pl.ds(i * 64 + 32, 32)
            right = jnp.concatenate([rp[0, back, ch], rp[1, back, ch], rtj[:, ch]], axis=0)
            tgv[rows, ch] = mm(low2[rows, :], right).astype(BF16)

    await_bytes(all_but_one, rt_sem.at[1])
    sums = [jnp.sum(rr2[k], axis=0) for k in range(4)]
    rg_out[...] = (sums[0] + sums[1]) + (sums[2] + sums[3])

    seven = send1.at[:, pl.ds(0, 112)]
    for ref, number in (
        (seven, 0), (seven, 1), (xs.at[:, 0], 2), (xs.at[:, pl.ds(0, 2)], 3),
        (rc, 5), (sx, 6), (seven, 7), (seven, 8),
        (rsend.at[pl.ds(0, 112)], 9), (all_but_one, 10),
    ):
        await_bytes(ref, snd_sem.at[number])


def store_kernel(tg, rg, g1, g2, tg_hbm, rg_out, g1_hbm, g2_hbm, sem):
    stores = [
        pltpu.make_async_copy(a, b, sem.at[i])
        for i, (a, b) in enumerate(((g1, g1_hbm), (g2, g2_hbm), (tg, tg_hbm)))
    ]
    for store in stores:
        store.start()
    rg_out[:, :HID] = rg[0:1, :]
    rg_out[:, HID:] = rg[1:2, :]
    for store in stores:
        store.wait()


def body(tokens, cotangent, router, first_weight, second_weight):
    vmem, dma = pltpu.VMEM, pltpu.SemaphoreType.DMA
    results = pl.pallas_call(
        kernel,
        out_shape=(
            vmem((IMG * TOK, DIM), BF16),
            vmem((2, HID), F32),
            vmem((DIM, HID), BF16),
            vmem((HID, DIM), BF16),
        ),
        in_specs=[pl.BlockSpec(memory_space=pltpu.HBM)] * 5,
        out_specs=(pl.BlockSpec(memory_space=pltpu.VMEM),) * 4,
        scratch_shapes=[
            vmem((IMG * TOK, DIM), BF16),
            vmem((IMG * TOK, DIM), BF16),
            vmem((EXP, DIM), BF16),
            vmem((EXP, DIM), BF16),
            vmem((DIM, HID), BF16),
            vmem((HID, DIM), BF16),
            vmem((256, 1024), BF16),
            vmem((IMG * TOK, EXP), F32),
            vmem((IMG * TOK, EXP), F32),
            vmem((IMG * TOK, EXP), BF16),
            vmem((128, 128), BF16),
            vmem((128, 128), BF16),
            vmem((UNITS, 128, CW), BF16),
            vmem((UNITS, 128, CW), BF16),
            vmem((UNITS, 2, 64, CW), BF16),
            vmem((UNITS, N_BLK, 2, 64, CW), BF16),
            vmem((2, 256, HID), F32),
            vmem((2, 256, HID), F32),
            vmem((2, 256, HID), BF16),
            vmem((2, 256, HID), BF16),
            vmem((UNITS, N_BLK, 2, 64, CW), BF16),
            vmem((UNITS, 2, 2, 64, CW), BF16),
            vmem((UNITS, 2, 64, CW), F32),
            vmem((UNITS, 2, 64, CW), BF16),
            vmem((UNITS, 2, 64, CW), BF16),
            vmem((UNITS, 2, 64, CW), BF16),
            vmem((UNITS, 2, 64, CW), BF16),
            vmem((UNITS, 128, CW), BF16),
            vmem((UNITS, 128, CW), BF16),
            vmem((2, 128, DIM), BF16),
            vmem((2, IMG * TOK, EXP), F32),
            vmem((2, IMG * TOK, EXP), F32),
            vmem((IMG * TOK, 2 * EXP), BF16),
            vmem((NZ * 16, HID), BF16),
            vmem((NZ * 16, HID), BF16),
            vmem((NYX, 2, HID), F32),
            vmem((4, NZ, 2, HID), F32),
            vmem((32, 2, HID), F32),
            dma((5,)),
            dma((UNITS,)), dma((UNITS,)), dma((UNITS,)), dma((UNITS,)),
            dma((UNITS,)), dma((UNITS,)), dma((UNITS,)), dma((UNITS,)),
            dma((3,)), dma((12,)),
        ],
        compiler_params=pltpu.CompilerParams(
            collective_id=0, has_side_effects=True, vmem_limit_bytes=56 * 1024 * 1024
        ),
    )(
        tokens.reshape(IMG * TOK, DIM), cotangent.reshape(IMG * TOK, DIM), router.T,
        first_weight[0], second_weight[0],
    )
    token_grad, router_column, first_grad, second_grad = pl.pallas_call(
        store_kernel,
        out_shape=(
            jax.ShapeDtypeStruct((IMG * TOK, DIM), BF16),
            jax.ShapeDtypeStruct((1, DIM), F32),
            jax.ShapeDtypeStruct((DIM, HID), BF16),
            jax.ShapeDtypeStruct((HID, DIM), BF16),
        ),
        in_specs=[pl.BlockSpec(memory_space=pltpu.VMEM)] * 4,
        out_specs=(
            pl.BlockSpec(memory_space=pl.ANY),
            pl.BlockSpec(memory_space=pltpu.VMEM),
            pl.BlockSpec(memory_space=pl.ANY),
            pl.BlockSpec(memory_space=pl.ANY),
        ),
        scratch_shapes=[dma((3,))],
        compiler_params=pltpu.CompilerParams(vmem_limit_bytes=8 * 1024 * 1024),
    )(*results)
    return (
        token_grad.reshape(IMG, TOK, DIM),
        router_column.reshape(DIM, 1),
        first_grad[None],
        second_grad[None],
    )


def solution(mesh):
    placed = (
        P(("dp", "expert"), None, None),
        P(("dp", "expert"), None, None),
        P(),
        P("expert", None, "dp"),
        P("expert", "dp", None),
    )
    return jax.shard_map(
        body,
        mesh=mesh,
        in_specs=placed,
        out_specs=(
            P(("dp", "expert"), None, None),
            P(None, "expert"),
            P("expert", None, "dp"),
            P("expert", "dp", None),
        ),
        check_vma=False,
    )
```

```python
import functools

import jax
import jax.numpy as jnp
from jax import lax
from jax.experimental import pallas as pl
from jax.experimental.pallas import tpu as pltpu
from jax.sharding import PartitionSpec as P

ROOT_TWO_OVER_PI = 0.7978845608028654
CUBIC_TERM = 0.044715
MESH = pl.DeviceIdType.MESH
F32, BF16 = jnp.float32, jnp.bfloat16

NZ, NYX = 8, 8
IMG, TOK, DIM, HID, EXP = 2, 256, 1280, 640, 64
CW = 256
NC = DIM // CW
N_BLK = 4
UNITS = 2 * NC
LAST = 38


def mm(a, b):
    return lax.dot_general(a, b, (((1,), (0,)), ((), ())), preferred_element_type=F32)


def mm_nt(a, b):
    return lax.dot_general(a, b, (((1,), (1,)), ((), ())), preferred_element_type=F32)


def mm_tn(a, b):
    return lax.dot_general(a, b, (((0,), (0,)), ((), ())), preferred_element_type=F32)


def iota(shape, axis):
    return lax.broadcasted_iota(jnp.int32, shape, axis)


def one_hot(mask):
    return jnp.where(mask, 1.0, 0.0).astype(BF16)


def kernel(
    tok_hbm, cot_hbm, rt_hbm, w1_hbm, w2_hbm,
    tgv, rg_out, g1v, g2v,
    tok, cot, rt, rtj, w1, w2, ltm, disp, comb, dlow, perm1, perm3,
    send1, recv1, send2, xs, acc_pre, acc_act, hid, pg,
    op, rc, t_own, sx, rx, so, ry, sz, rz, rp, cgx, dgx, low2,
    rsend, rrecv, rs2, rr2, rr3,
    in_sem, z1_sem, y1_sem, agx_sem, agc_sem,
    rc_sem, rx_sem, ry_sem, rz_sem, rt_sem, snd_sem,
):
    p = lax.axis_index("dp")
    q = lax.axis_index("expert")
    z = lax.rem(q, NZ)
    yx = lax.div(q, NZ)
    y = lax.div(yx, 2)
    xh = lax.rem(yx, 2)

    z_at = [lax.rem(z + far, NZ) for far in (4, 3, 5, 2, 6, 1, 7)]
    z_peers = [(zt, (p, yx * NZ + zt)) for zt in z_at]
    p_flip = lax.rem(p + 2, 4)
    p_at, xh_at = (p, p_flip), (xh, 1 - xh)

    def yx_peer(dy, dx):
        yxt = lax.rem(y + dy, 4) * 2 + xh_at[dx]
        return yxt, (p_at[dx], yxt * NZ + z)

    yx_peers = [yx_peer(k // 2, k % 2) for k in range(1, 8)]
    core_peer = (p + 1 - 2 * lax.rem(p, 2), q)
    x_peer = (p_flip, q)
    dp_peers = [(lax.rem(p + k, 4), q) for k in range(1, 4)]

    def remote(src, dst, send_sem, recv_sem, dev):
        pltpu.make_async_remote_copy(
            src_ref=src, dst_ref=dst, send_sem=send_sem, recv_sem=recv_sem,
            device_id=dev, device_id_type=MESH,
        ).start()

    def await_bytes(ref, sem):
        pltpu.make_async_copy(ref, ref, sem).wait()

    def split(u):
        c = lax.rem(u, NC)
        return lax.div(u, NC), c, pl.ds(pl.multiple_of(c * CW, CW), CW)

    def rows_at(index, size):
        return pl.ds(pl.multiple_of(index * size, size), size)

    loads = [
        pltpu.make_async_copy(a, b, in_sem.at[i])
        for i, (a, b) in enumerate(
            ((rt_hbm, rt), (tok_hbm, tok), (cot_hbm, cot), (w1_hbm, w1), (w2_hbm, w2))
        )
    ]
    for load in loads[:3]:
        load.start()

    barrier = pltpu.get_barrier_semaphore()

    column = [(pt, yx * NZ + zt) for zt in z_at for pt, _ in dp_peers]
    for dev in [dev for _, dev in z_peers + yx_peers] + dp_peers + column:
        pl.semaphore_signal(barrier, inc=1, device_id=dev, device_id_type=MESH)

    o1, n1 = iota((128, 128), 0), iota((128, 128), 1)
    perm1[...] = one_hot(
        n1 == ((o1 >> 1) & 7) * 16 + ((o1 >> 4) & 3) * 4 + (o1 >> 6) * 2 + (o1 & 1)
    )
    perm3[...] = one_hot(n1 == (o1 & 31) * 4 + ((o1 >> 5) & 1) * 2 + (o1 >> 6))

    def expert_of(j):
        y_at = (y + (j >> 5) * 2 + ((j >> 1) & 1)) & 3
        return (y_at * 2 + ((xh + j) & 1)) * 8 + ((j >> 2) & 7)

    n2, j2 = iota((256, EXP), 0), iota((256, EXP), 1)
    same_slot = j2 == n2 >> 2

    loads[0].wait()
    by_slot = one_hot(iota((EXP, EXP), 1) == expert_of(iota((EXP, EXP), 0)))
    rtj[...] = mm(by_slot, rt[...]).astype(BF16)
    loads[1].wait()
    loads[3].start()
    loads[4].start()
    logits = mm_nt(tok[...], rtj[...])
    for i in range(IMG):
        rows = pl.ds(i * TOK, TOK)
        part = logits[i * TOK:(i + 1) * TOK]
        up = jnp.exp(part - jnp.max(part, axis=0, keepdims=True))
        d = up / jnp.sum(up, axis=0, keepdims=True)
        up = jnp.exp(part - jnp.max(part, axis=1, keepdims=True))
        c = up / jnp.sum(up, axis=1, keepdims=True)
        disp[rows, :] = d
        comb[rows, :] = c
        d_low = d.astype(BF16)
        dlow[rows, :] = d_low
        for a, low in ((0, d_low), (1, c.astype(BF16))):
            spread = one_hot(same_slot & ((n2 & 3) == a * 2 + i))
            ltm[:, pl.ds(a * 512 + i * TOK, TOK)] = mm_nt(spread, low).astype(BF16)
    loads[2].wait()
    pl.semaphore_wait(barrier, 38)

    def send_slots(u):
        h, c, ch = split(u)
        rows = rows_at(h, 128)
        send1[u] = (
            mm(ltm[rows, :512], tok[:, ch]) + mm(ltm[rows, 512:], cot[:, ch])
        ).astype(BF16)
        mine = rows_at(z, 16)
        recv1[u, mine] = send1[u, mine]

        for zt, dev in z_peers:
            remote(
                send1.at[u, rows_at(zt, 16)], recv1.at[u, mine],
                snd_sem.at[0], z1_sem.at[u], dev,
            )

    def to_neighbours(h, src, dst, send_sem, recv_sem, sign):
        @pl.when(h == 1)
        def _():
            remote(src(0), dst(0), send_sem, recv_sem, yx_peer(2, 0)[1])

        start = 2 * h if sign > 0 else 8 - 2 * h
        for k in (3, 2, 1):
            remote(src(k), dst(k), send_sem, recv_sem, yx_peer(start + sign * (k // 2), k % 2)[1])

    def await_neighbours(h, ref, sem):
        @pl.when(h == 0)
        def _():
            await_bytes(ref.at[:, pl.ds(0, 48)], sem)

        @pl.when(h == 1)
        def _():
            await_bytes(ref, sem)

    def turn_slots(u):
        h, c, ch = split(u)
        await_bytes(recv1.at[u, pl.ds(0, 112)], z1_sem.at[u])
        send2[u] = mm(perm1[...], recv1[u]).astype(BF16).reshape(2, 64, CW)

        @pl.when(h == 0)
        def _():
            xs[u, 0, :, :16] = send2[u, :, :16]

        to_neighbours(
            h, lambda k: send2.at[u, :, rows_at(k, 16)],
            lambda k: xs.at[u, 0, :, rows_at(k, 16)], snd_sem.at[1], y1_sem.at[u], 1,
        )

    def gather_slots(u):
        h, c, ch = split(u)
        await_neighbours(h, xs.at[u, 0], y1_sem.at[u])
        remote(xs.at[u, 0], xs.at[u, 1], snd_sem.at[2], agx_sem.at[u], x_peer)

    def forward_slots(u):
        h, c, ch = split(u)
        await_bytes(xs.at[u, 1], agx_sem.at[u])
        remote(
            xs.at[u, pl.ds(0, 2)], xs.at[u, pl.ds(2, 2)], snd_sem.at[3], agc_sem.at[u], core_peer
        )

    def first_layer(u):
        h, c, ch = split(u)
        await_bytes(xs.at[u, pl.ds(2, 2)], agc_sem.at[u])
        acc_pre[h] += mm(xs[u, :, 0].reshape(256, CW), w1[ch, :])
        acc_act[h] += mm_nt(xs[u, :, 1].reshape(256, CW), w2[:, ch])

        @pl.when(c == NC - 1)
        def _():
            @pl.loop(0, 4)
            def _(b):
                rows = rows_at(b, 64)
                v = acc_pre[h, rows, :]
                square = v * v
                tangent = jnp.tanh(ROOT_TWO_OVER_PI * (v + CUBIC_TERM * square * v))
                hid[h, rows, :] = (0.5 * v * (1.0 + tangent)).astype(BF16)
                slope = 0.5 * (1.0 + tangent) + 0.5 * v * (
                    1.0 - tangent * tangent
                ) * ROOT_TWO_OVER_PI * (1.0 + 3.0 * CUBIC_TERM * square)
                pg[h, rows, :] = (acc_act[h, rows, :] * slope).astype(BF16)

    def second_layer(u):
        h, c, ch = split(u)
        op[u, :, 0] = mm(hid[h], w2[:, ch]).astype(BF16).reshape(N_BLK, 64, CW)
        op[u, :, 1] = mm_nt(pg[h], w1[ch, :]).astype(BF16).reshape(N_BLK, 64, CW)
        remote(
            op.at[u, pl.ds(2, 2)], rc.at[u],
            snd_sem.at[5], rc_sem.at[u], core_peer,
        )

    def core_sum(u):
        h, c, ch = split(u)
        await_bytes(rc.at[u], rc_sem.at[u])
        sx[u] = (
            op[u, 1].astype(F32) + rc[u, 1].astype(F32)
        ).astype(BF16)
        remote(sx.at[u], rx.at[u], snd_sem.at[6], rx_sem.at[u], x_peer)
        t_own[u] = op[u, 0].astype(F32) + rc[u, 0].astype(F32)

    def weight_grads(c):
        ch = pl.ds(pl.multiple_of(c * CW, CW), CW)
        g1v[ch, :] = (
            mm_tn(xs[c, :, 0].reshape(256, CW), pg[0])
            + mm_tn(xs[NC + c, :, 0].reshape(256, CW), pg[1])
        ).astype(BF16)
        g2v[:, ch] = (
            mm_tn(hid[0], xs[c, :, 1].reshape(256, CW))
            + mm_tn(hid[1], xs[NC + c, :, 1].reshape(256, CW))
        ).astype(BF16)

    def x_sum(u):
        h, c, ch = split(u)
        await_bytes(rx.at[u], rx_sem.at[u])
        so[u] = (t_own[u] + rx[u].astype(F32)).astype(BF16)

        @pl.when(h == 0)
        def _():
            ry[u, :, :16] = so[u, :, :16]

        to_neighbours(
            h, lambda k: so.at[u, :, rows_at(k, 16)],
            lambda k: ry.at[u, :, rows_at(k, 16)], snd_sem.at[7], ry_sem.at[u], -1,
        )

    def turn_back(u):
        h, c, ch = split(u)
        await_neighbours(h, ry.at[u], ry_sem.at[u])
        sz[u] = mm_tn(perm1[...], ry[u].reshape(128, CW)).astype(BF16)
        mine = rows_at(z, 16)
        rz[u, mine] = sz[u, mine]

        for zt, dev in z_peers:
            remote(
                sz.at[u, rows_at(zt, 16)], rz.at[u, mine],
                snd_sem.at[8], rz_sem.at[u], dev,
            )

    def slots_back(u):
        h, c, ch = split(u)
        await_bytes(rz.at[u, pl.ds(0, 112)], rz_sem.at[u])
        rp[h, :, ch] = mm(perm3[...], rz[u]).astype(BF16)
        for i in range(IMG):
            rows = pl.ds(i * TOK, TOK)
            slots = rp[h, pl.ds(i * 64, 64), ch]
            cgx[h, rows, :] += mm_nt(cot[rows, ch], slots)
            dgx[h, rows, :] += mm_nt(tok[rows, ch], slots)

    @pl.loop(0, LAST)
    def _(step):
        for lag, count, stage in (
            (0, UNITS, send_slots), (16, UNITS, second_layer), (23, UNITS, turn_back),
            (7, UNITS, gather_slots), (20, UNITS, x_sum), (4, UNITS, turn_slots),
            (28, UNITS, slots_back), (31, NC, weight_grads), (10, UNITS, forward_slots),
            (17, UNITS, core_sum), (11, UNITS, first_layer),
        ):
            @pl.when((step >= lag) & (step < lag + count))
            def _(stage=stage, lag=lag):
                stage(step - lag)

        @pl.when(step == 0)
        def _():
            for ref in (acc_pre, acc_act, cgx, dgx):
                ref[...] = jnp.zeros_like(ref)
            loads[3].wait()
            loads[4].wait()

    c_grads = jnp.concatenate([cgx[0, :, :32], cgx[1, :, :32]], axis=1)
    d_grads = jnp.concatenate([dgx[0, :, 32:], dgx[1, :, 32:]], axis=1)
    for i in range(IMG):
        rows = pl.ds(i * TOK, TOK)
        d, c = disp[rows, :], comb[rows, :]
        d_grad, c_grad = d_grads[i * TOK:(i + 1) * TOK], c_grads[i * TOK:(i + 1) * TOK]
        grad = d * (d_grad - jnp.sum(d * d_grad, axis=0, keepdims=True))
        grad = grad + c * (c_grad - jnp.sum(c * c_grad, axis=1, keepdims=True))
        low2[rows, :64] = dlow[rows, :]
        low2[rows, 64:] = grad.astype(BF16)

    all_but_one = rr3.at[pl.ds(0, 31)]

    r3, j3 = iota((EXP, EXP), 1), iota((EXP, EXP), 0)
    by_peer = one_hot(j3 == (r3 >> 5) * 32 + (r3 & 7) * 4 + ((r3 >> 3) & 3))
    turned = mm(low2[:, 64:], by_peer).astype(BF16)
    part = mm_tn(turned, tok[...])
    for k in range(NYX):
        rows = part[k * 8:(k + 1) * 8]
        rsend[pl.ds(k * 16, 16), :] = jnp.concatenate(
            [rows[:, :HID], rows[:, HID:]], axis=0
        ).astype(BF16)
    for k in (5, 4, 3, 7, 2, 6, 1):
        dev = yx_peers[k - 1][1]
        rows = pl.ds(k * 16, 16)
        remote(rsend.at[rows], rrecv.at[rows], snd_sem.at[9], rt_sem.at[0], dev)

    await_bytes(rrecv.at[pl.ds(16, 112)], rt_sem.at[0])
    total = rsend[pl.ds(0, 16), :].astype(F32)
    for k in range(1, NYX):
        total = total + rrecv[pl.ds(k * 16, 16), :].astype(F32)
    for k in range(NZ):
        rs2[k, pl.ds(0, 1), :] = total[k:k + 1]
        rs2[k, pl.ds(1, 1), :] = total[8 + k:9 + k]
    for zt in z_at + [z]:
        for pt in [pt for pt, _ in dp_peers] + [p]:
            if zt is not z or pt is not p:
                remote(
                    rs2.at[zt], rr2.at[p, z], snd_sem.at[10], rt_sem.at[1], (pt, yx * NZ + zt)
                )
    rr2[p, z] = rs2[z]

    for i in range(IMG):
        rows = pl.ds(i * TOK, TOK)

        @pl.loop(0, NC)
        def _(c, i=i, rows=rows):
            ch = pl.ds(pl.multiple_of(c * CW, CW), CW)
            back = pl.ds(i * 64 + 32, 32)
            right = jnp.concatenate([rp[0, back, ch], rp[1, back, ch], rtj[:, ch]], axis=0)
            tgv[rows, ch] = mm(low2[rows, :], right).astype(BF16)

    await_bytes(all_but_one, rt_sem.at[1])
    sums = [jnp.sum(rr2[k], axis=0) for k in range(4)]
    rg_out[...] = (sums[0] + sums[1]) + (sums[2] + sums[3])

    seven = send1.at[:, pl.ds(0, 112)]
    for ref, number in (
        (seven, 0), (seven, 1), (xs.at[:, 0], 2), (xs.at[:, pl.ds(0, 2)], 3),
        (rc, 5), (sx, 6), (seven, 7), (seven, 8),
        (rsend.at[pl.ds(0, 112)], 9), (all_but_one, 10),
    ):
        await_bytes(ref, snd_sem.at[number])


def store_kernel(tg, rg, g1, g2, tg_hbm, rg_out, g1_hbm, g2_hbm, sem):
    stores = [
        pltpu.make_async_copy(a, b, sem.at[i])
        for i, (a, b) in enumerate(((g1, g1_hbm), (g2, g2_hbm), (tg, tg_hbm)))
    ]
    for store in stores:
        store.start()
    rg_out[:, :HID] = rg[0:1, :]
    rg_out[:, HID:] = rg[1:2, :]
    for store in stores:
        store.wait()


def body(tokens, cotangent, router, first_weight, second_weight):
    vmem, dma = pltpu.VMEM, pltpu.SemaphoreType.DMA
    results = pl.pallas_call(
        kernel,
        out_shape=(
            vmem((IMG * TOK, DIM), BF16),
            vmem((2, HID), F32),
            vmem((DIM, HID), BF16),
            vmem((HID, DIM), BF16),
        ),
        in_specs=[pl.BlockSpec(memory_space=pltpu.HBM)] * 5,
        out_specs=(pl.BlockSpec(memory_space=pltpu.VMEM),) * 4,
        scratch_shapes=[
            vmem((IMG * TOK, DIM), BF16),
            vmem((IMG * TOK, DIM), BF16),
            vmem((EXP, DIM), BF16),
            vmem((EXP, DIM), BF16),
            vmem((DIM, HID), BF16),
            vmem((HID, DIM), BF16),
            vmem((256, 1024), BF16),
            vmem((IMG * TOK, EXP), F32),
            vmem((IMG * TOK, EXP), F32),
            vmem((IMG * TOK, EXP), BF16),
            vmem((128, 128), BF16),
            vmem((128, 128), BF16),
            vmem((UNITS, 128, CW), BF16),
            vmem((UNITS, 128, CW), BF16),
            vmem((UNITS, 2, 64, CW), BF16),
            vmem((UNITS, N_BLK, 2, 64, CW), BF16),
            vmem((2, 256, HID), F32),
            vmem((2, 256, HID), F32),
            vmem((2, 256, HID), BF16),
            vmem((2, 256, HID), BF16),
            vmem((UNITS, N_BLK, 2, 64, CW), BF16),
            vmem((UNITS, 2, 2, 64, CW), BF16),
            vmem((UNITS, 2, 64, CW), F32),
            vmem((UNITS, 2, 64, CW), BF16),
            vmem((UNITS, 2, 64, CW), BF16),
            vmem((UNITS, 2, 64, CW), BF16),
            vmem((UNITS, 2, 64, CW), BF16),
            vmem((UNITS, 128, CW), BF16),
            vmem((UNITS, 128, CW), BF16),
            vmem((2, 128, DIM), BF16),
            vmem((2, IMG * TOK, EXP), F32),
            vmem((2, IMG * TOK, EXP), F32),
            vmem((IMG * TOK, 2 * EXP), BF16),
            vmem((NZ * 16, HID), BF16),
            vmem((NZ * 16, HID), BF16),
            vmem((NYX, 2, HID), F32),
            vmem((4, NZ, 2, HID), F32),
            vmem((32, 2, HID), F32),
            dma((5,)),
            dma((UNITS,)), dma((UNITS,)), dma((UNITS,)), dma((UNITS,)),
            dma((UNITS,)), dma((UNITS,)), dma((UNITS,)), dma((UNITS,)),
            dma((3,)), dma((12,)),
        ],
        compiler_params=pltpu.CompilerParams(
            collective_id=0, has_side_effects=True, vmem_limit_bytes=56 * 1024 * 1024
        ),
    )(
        tokens.reshape(IMG * TOK, DIM), cotangent.reshape(IMG * TOK, DIM), router.T,
        first_weight[0], second_weight[0],
    )
    token_grad, router_column, first_grad, second_grad = pl.pallas_call(
        store_kernel,
        out_shape=(
            jax.ShapeDtypeStruct((IMG * TOK, DIM), BF16),
            jax.ShapeDtypeStruct((1, DIM), F32),
            jax.ShapeDtypeStruct((DIM, HID), BF16),
            jax.ShapeDtypeStruct((HID, DIM), BF16),
        ),
        in_specs=[pl.BlockSpec(memory_space=pltpu.VMEM)] * 4,
        out_specs=(
            pl.BlockSpec(memory_space=pl.ANY),
            pl.BlockSpec(memory_space=pltpu.VMEM),
            pl.BlockSpec(memory_space=pl.ANY),
            pl.BlockSpec(memory_space=pl.ANY),
        ),
        scratch_shapes=[dma((3,))],
        compiler_params=pltpu.CompilerParams(vmem_limit_bytes=8 * 1024 * 1024),
    )(*results)
    return (
        token_grad.reshape(IMG, TOK, DIM),
        router_column.reshape(DIM, 1),
        first_grad[None],
        second_grad[None],
    )


def solution(mesh):
    placed = (
        P(("dp", "expert"), None, None),
        P(("dp", "expert"), None, None),
        P(),
        P("expert", None, "dp"),
        P("expert", "dp", None),
    )
    return jax.shard_map(
        body,
        mesh=mesh,
        in_specs=placed,
        out_specs=(
            P(("dp", "expert"), None, None),
            P(None, "expert"),
            P("expert", None, "dp"),
            P("expert", "dp", None),
        ),
        check_vma=False,
    )
```
